128 devices in a mesh: ctx: 16 (over y, z), chan: 8 (over x, core).
Axes of the slice: x: 4, y: 4, z: 4, core: 2. Of those that a mesh axis runs over, the one named last changes fastest.
Arguments:
- tokens: bfloat16 [4096, 4096], P('ctx', 'chan'), may hold values from -6 to 6
- w_in: bfloat16 [4096, 3, 4096], P(None, None, 'chan'), may hold values from -0.09375 to 0.09375
- short_kernel: float32 [3, 3, 4096], P(None, None, 'chan'), may hold values from -3 to 3
- residue: float32 [4096, 16], P('chan'), may hold values from -2 to 2
- rate: float32 [4096, 16], P('chan'), as said below
- w_out: bfloat16 [4096, 4096], P(None, 'chan'), may hold values from -0.09375 to 0.09375
Outputs:
- mixed: bfloat16 [4096, 4096], P('ctx', 'chan')
The draws below stay inside these ranges and needn't reach their ends.
Inputs may be any that keep to these rules, and one draw needn't show every extreme that they name: `rate`: all rates are positive.
All inputs are finite; a program needn't handle non-finite values.
Results may differ from the reference program's by a relative error of at most 0.0074.
Values may be sent and summed in bfloat16 or wider, within the bound.
A program may use at most 128 MiB of HBM per device.

```python
import jax
import jax.numpy as jnp
from jax import lax

D = 4096
MODES = 16
SHORT = 3
TOKENS = 4096


def draw_rate(key, part):
    key = jax.random.fold_in(key, 11)
    pick_key, slow_key, fast_key = jax.random.split(key, 3)
    share = 0.5
    slow_flag = jax.random.bernoulli(pick_key, share, (D, 1))
    lowest = jnp.log(0.25 / TOKENS)
    highest = jnp.log(2.0 / TOKENS)
    slow = jnp.exp(jax.random.uniform(slow_key, (D, MODES), jnp.float32, lowest, highest))
    fast = jax.random.uniform(fast_key, (D, MODES), jnp.float32, 1.0 / 50.0, 1.0 / 30.0)
    return jnp.where(slow_flag, slow, fast).astype(jnp.float32)


def level_of(key, extent, pieces, smallest, largest):
    loudness = 1.0
    for dim, shards_of in pieces:
        steps = jax.random.uniform(jax.random.fold_in(jax.random.fold_in(key, 6), dim), (shards_of,), jnp.float32, smallest / len(pieces), largest / len(pieces))
        loudness = loudness * jnp.repeat(jnp.exp(steps), extent[dim] // shards_of).reshape((-1,) + (1,) * (len(extent) - 1 - dim))
    return loudness


def gaussian(rng, extent, scale, limit, shards=(), kind=jnp.bfloat16):
    factor_of = level_of(rng, extent, shards, -0.22, 0.18) if shards else 1.0
    result = jax.random.normal(rng, extent, jnp.float32) * scale * factor_of
    return jnp.minimum(jnp.maximum(result, -limit), limit).astype(kind)


def setup_inputs(seed: int = 0) -> dict:
    seeds = jax.random.split(jax.random.key(seed), 7)
    tokens = gaussian(seeds[0], (TOKENS, D), 1.0, 6.0, ((0, 16), (1, 8)))
    w_in = gaussian(seeds[1], (D, 3, D), D ** -0.5, 0.09375, ((2, 8),))
    short_kernel = gaussian(seeds[2], (SHORT, 3, D), 0.6, 3.0, ((2, 8),), jnp.float32)
    residue = gaussian(seeds[3], (D, MODES), 0.25, 2.0, ((0, 8),), jnp.float32)
    rate = draw_rate(jax.random.fold_in(seeds[6], 71), 0)
    w_out = gaussian(seeds[5], (D, D), D ** -0.5, 0.09375, ((1, 8),))
    return dict(tokens=tokens, w_in=w_in, short_kernel=short_kernel, residue=residue, rate=rate, w_out=w_out)


def reference(tokens, w_in, short_kernel, residue, rate, w_out):
    projected = jnp.dot(tokens, w_in.reshape(D, 3 * D), preferred_element_type=jnp.float32).astype(jnp.bfloat16)
    projected = projected.reshape(TOKENS, 3, D)
    padded = jnp.concatenate([jnp.zeros((SHORT - 1, 3, D), jnp.bfloat16), projected], 0)
    filtered = jnp.zeros((TOKENS, 3, D), jnp.float32)
    for tap in range(SHORT):
        first = SHORT - 1 - tap
        filtered = filtered + short_kernel[tap] * padded[first:first + TOKENS].astype(jnp.float32)
    gated = (filtered[:, 1] * filtered[:, 2]).astype(jnp.bfloat16)
    decay = jnp.exp(-rate)
    weight = residue * jnp.sqrt(1.0 - jnp.exp(-2.0 * rate))

    def advance(state, token_row):
        state = decay * state + token_row.astype(jnp.float32)[:, None]
        return (state, lax.optimization_barrier(jnp.sum(weight * state, axis=1)))
    unused_state, long_conv = lax.scan(advance, jnp.zeros((D, MODES), jnp.float32), gated)
    modulated = (filtered[:, 0] * long_conv).astype(jnp.bfloat16)
    return jnp.dot(modulated, w_out, preferred_element_type=jnp.float32).astype(jnp.bfloat16)
```

```python
import functools

import jax
import jax.numpy as jnp
from jax import lax
from jax.experimental import pallas as pl
from jax.experimental.pallas import tpu as pltpu
from jax.sharding import PartitionSpec as P

MESH = pl.DeviceIdType.MESH
F32 = jnp.float32
BF16 = jnp.bfloat16
CTX = 16
ROWS = 256
WIDE = 512
BLOCKS = 8
MODES = 16
SHORT = 3
SUB = 32
LANES = 128
TILES = WIDE // LANES
PARTS = 2
PART = WIDE // PARTS
PAD = 8


def gather(ring, part_of, store, sems):
    block, left, right, far, dev = ring
    send, recv, base = sems
    count = [base]

    def copy(src, dst, where):
        s = count[0]
        count[0] += 1
        return pltpu.make_async_remote_copy(
            src_ref=src, dst_ref=dst, send_sem=send.at[s], recv_sem=recv.at[s],
            device_id=where, device_id_type=MESH)

    def here(owner, part):
        return store.at[owner, :, pl.ds(part * PART, PART)]

    to_right, to_left, to_other = dev(1), dev(3), dev(0, True)
    out_r = [copy(part_of(c), here(block, c), to_right) for c in range(PARTS)]
    out_l = [copy(part_of(c), here(block, c), to_left) for c in range(PARTS)]
    own = [copy(part_of(c), here(block, c), to_other) for c in range(PARTS)]
    fwd_r = copy(here(left, 0), here(left, 0), to_right)
    fwd_l = copy(here(right, 1), here(right, 1), to_left)
    side_l = [copy(here(left, c), here(left, c), to_other) for c in range(PARTS)]
    side_r = [copy(here(right, c), here(right, c), to_other) for c in range(PARTS)]
    side_f = [copy(here(far, c), here(far, c), to_other) for c in range(PARTS)]
    return dict(out_r=out_r, out_l=out_l, own=own, fwd_r=fwd_r, fwd_l=fwd_l,
                side_l=side_l, side_r=side_r, side_f=side_f)


def relay(g, first, near, last):
    first()
    g["out_r"][0].wait_recv()
    g["fwd_r"].start()
    g["side_l"][0].start()
    g["out_l"][1].wait_recv()
    g["fwd_l"].start()
    g["side_r"][1].start()
    near[0]()
    g["out_r"][1].wait_recv()
    g["side_l"][1].start()
    g["out_l"][0].wait_recv()
    g["side_r"][0].start()
    near[1]()
    for c in range(PARTS):
        g["side_l"][c].wait_recv()
        g["side_r"][c].wait_recv()
    near[2]()
    g["fwd_r"].wait_recv()
    g["side_f"][0].start()
    g["fwd_l"].wait_recv()
    g["side_f"][1].start()
    last[0]()
    for c in range(PARTS):
        g["side_f"][c].wait_recv()
    last[1]()


def finish(g):
    for name in ("out_r", "out_l", "own", "side_l", "side_r", "side_f"):
        for c in g[name]:
            c.wait_send()
    g["fwd_r"].wait_send()
    g["fwd_l"].wait_send()


def kernel(tok, w_in, taps, residue, rate, w_out, out,
           win, wout, gat, mod, acc, total, gated, conv, gate0, decay, weight, entry_sub, ramp,
           tail_out, tail_in, state_out, state_in,
           w_sems, o_sems, own_sem, send1, recv1, send2, recv2, tail_send, tail_recv, st_send, st_recv):
    me = lax.axis_index("chan")
    ctx = lax.axis_index("ctx")
    x, core = me // 2, me % 2

    def at(step, flip=False):
        return lax.rem(x + step, 4) * 2 + (1 - core if flip else core)

    def dev(step, flip=False):
        return (ctx, at(step, flip))

    order = [me, at(0, True), at(3), at(1), at(3, True), at(1, True), at(2), at(2, True)]

    load_w = [pltpu.make_async_copy(w_in.at[:, b], win.at[:, b], w_sems.at[n]) for n, b in enumerate(order)]
    load_o = [pltpu.make_async_copy(w_out.at[b], wout.at[b], o_sems.at[n]) for n, b in enumerate(order)]
    load_t = pltpu.make_async_copy(tok, gat.at[me], own_sem)

    barrier = pltpu.get_barrier_semaphore()
    for d in (dev(1), dev(3), dev(0, True)):
        pl.semaphore_signal(barrier, inc=1, device_id=d, device_id_type=MESH)
    for back in range(1, CTX):
        @pl.when(ctx >= back)
        def _():
            pl.semaphore_signal(barrier, inc=1, device_id=(ctx - back, me), device_id_type=MESH)
    load_t.start()
    load_w[0].start()
    load_w[1].start()
    pl.semaphore_wait(barrier, 3 + CTX - 1 - ctx)

    ring = (me, at(3), at(1), at(2), dev)
    g1 = gather(ring, lambda c: tok.at[:, pl.ds(c * PART, PART)], gat, (send1, recv1, 0))
    g1["out_r"][0].start()
    g1["out_l"][1].start()
    g1["out_r"][1].start()
    g1["out_l"][0].start()
    for c in range(PARTS):
        g1["own"][c].start()
    for n in range(2, BLOCKS):
        load_w[n].start()
    for n in range(BLOCKS):
        load_o[n].start()

    dec = jnp.exp(-rate[...])
    decay[0] = dec
    for n, power in enumerate((8, 32, 64, 128, 256)):
        decay[n + 1] = jnp.exp(-rate[...] * float(power))
    weight[...] = residue[...] * jnp.sqrt(1.0 - jnp.exp(-2.0 * rate[...]))
    steps = lax.broadcasted_iota(jnp.int32, (8, WIDE), 0).astype(F32) + 1.0
    for r in range(MODES):
        ramp[r] = jnp.exp(-rate[r:r + 1] * steps) * weight[r:r + 1]

    def project(n, fresh=False, slots=(0, 1, 2)):
        b = order[n]
        load_w[n].wait()
        for s in slots:
            part = jnp.dot(gat[b], win[s, b], preferred_element_type=F32)
            if fresh:
                acc[s, PAD:PAD + ROWS] = part
            else:
                acc[s, PAD:PAD + ROWS] += part

    def do_first():
        load_t.wait()
        project(0, True)

    def do_sibling():
        for c in range(PARTS):
            g1["own"][c].wait_recv()
        project(1)

    def do_near():
        project(2)
        project(3)

    def do_near_other():
        project(4)
        project(5)

    relay(g1, do_first, (do_sibling, do_near, do_near_other),
          (lambda: project(6), lambda: project(7)))

    for s in range(3):
        tail_out[2 * s:2 * s + 2] = acc[s, PAD + ROWS - 2:PAD + ROWS].astype(BF16).astype(F32)
    tail = pltpu.make_async_remote_copy(
        src_ref=tail_out, dst_ref=tail_in, send_sem=tail_send.at[0], recv_sem=tail_recv.at[0],
        device_id=(lax.rem(ctx + 1, CTX), me), device_id_type=MESH)

    @pl.when(ctx < CTX - 1)
    def _():
        tail.start()

    for s in range(3):
        for q in range(8):
            rows = slice(PAD + SUB * q, PAD + SUB * (q + 1))
            acc[s, rows] = acc[s, rows].astype(BF16).astype(F32)

    @pl.when(ctx > 0)
    def _():
        tail.wait_recv()
        for s in range(3):
            acc[s, PAD - 2:PAD] = tail_in[2 * s:2 * s + 2]

    @pl.when(ctx == 0)
    def _():
        for s in range(3):
            acc[s, PAD - 2:PAD] = jnp.zeros((2, WIDE), F32)

    def filtered(s, q):
        value = None
        for tap in range(SHORT):
            first = PAD + SUB * q - tap
            term = taps[tap, s:s + 1] * acc[s, first:first + SUB]
            value = term if value is None else value + term
        return value

    def split(ref, q, value):
        for tile in range(TILES):
            ref[tile, SUB * q:SUB * (q + 1)] = value[:, tile * LANES:(tile + 1) * LANES]

    for q in range(8):
        split(gated, q, (filtered(1, q) * filtered(2, q)).astype(BF16).astype(F32))

    row = lax.broadcasted_iota(jnp.int32, (8, LANES), 0)

    def spread(ref, r, lanes):
        return jnp.broadcast_to(ref[r:r + 1, lanes], (8, LANES))

    @pl.loop(0, TILES)
    def _(tile):
        lanes = pl.ds(pl.multiple_of(tile * LANES, LANES), LANES)
        d = [spread(decay.at[0], r, lanes) for r in range(MODES)]

        def step(j, states):
            g = gated[tile, pl.ds(j, 8, stride=SUB)]
            return tuple(d[r] * states[r] + g for r in range(MODES))

        states = lax.fori_loop(0, SUB, step, tuple(jnp.zeros((8, LANES), F32) for _ in range(MODES)), unroll=4)
        for r in range(MODES):
            s = states[r]
            for n, shift in enumerate((1, 2, 4)):
                s = s + jnp.where(row >= shift, spread(decay.at[2 + n], r, lanes) * pltpu.roll(s, shift, 0), 0.0)
            state_out[r:r + 1, lanes] = s[7:8]
            entry_sub[r, :, lanes] = jnp.where(row >= 1, pltpu.roll(s, 1, 0), 0.0)

    for ahead in range(1, CTX):
        @pl.when(ctx + ahead < CTX)
        def _():
            pltpu.make_async_remote_copy(
                src_ref=state_out, dst_ref=state_in.at[ctx], send_sem=st_send.at[ahead], recv_sem=st_recv.at[ctx],
                device_id=(lax.rem(ctx + ahead, CTX), me), device_id_type=MESH).start()

    for q in range(8):
        split(gate0, q, filtered(0, q))

    @pl.loop(0, TILES)
    def _(tile):
        lanes = pl.ds(pl.multiple_of(tile * LANES, LANES), LANES)
        d = [spread(decay.at[0], r, lanes) for r in range(MODES)]
        w = [spread(weight, r, lanes) for r in range(MODES)]

        def step(j, states):
            g = gated[tile, pl.ds(j, 8, stride=SUB)]
            states = tuple(d[r] * states[r] + g for r in range(MODES))
            terms = [w[r] * states[r] for r in range(MODES)]
            while len(terms) > 1:
                terms = [a + b for a, b in zip(terms[::2], terms[1::2])]
            conv[tile, pl.ds(j, 8, stride=SUB)] = terms[0]
            return states

        lax.fori_loop(0, SUB, step, tuple(entry_sub[r, :, lanes] for r in range(MODES)), unroll=2)

    def merge(j, entry):
        pltpu.make_async_remote_copy(
            src_ref=state_out, dst_ref=state_in.at[j], send_sem=st_send.at[0], recv_sem=st_recv.at[j],
            device_id=(ctx, me), device_id_type=MESH).wait_recv()
        return decay[5] * entry + state_in[j]

    entry = lax.fori_loop(0, ctx, merge, jnp.zeros((MODES, WIDE), F32))
    state_in[CTX - 1] = entry

    def modulate(part):
        @pl.loop(part * PART // LANES, (part + 1) * PART // LANES)
        def _(tile):
            lanes = pl.ds(pl.multiple_of(tile * LANES, LANES), LANES)
            z = tuple(ramp[r, :, lanes] * state_in[CTX - 1, r:r + 1, lanes] for r in range(MODES))
            d8 = [spread(decay.at[1], r, lanes) for r in range(MODES)]

            def step(q, z):
                halves = []
                for half in range(2):
                    rows = pl.ds(pl.multiple_of(q * 16 + half * 8, 8), 8)
                    terms = list(z)
                    while len(terms) > 1:
                        terms = [a + b for a, b in zip(terms[::2], terms[1::2])]
                    halves.append(gate0[tile, rows] * (conv[tile, rows] + terms[0]))
                    z = tuple(d8[r] * z[r] for r in range(MODES))
                mod[me, pl.ds(pl.multiple_of(q * 16, 16), 16), lanes] = jnp.concatenate(halves, 0).astype(BF16)
                return z

            lax.fori_loop(0, ROWS // 16, step, z)

    g2 = gather(ring, lambda c: mod.at[me, :, pl.ds(c * PART, PART)], mod, (send2, recv2, 0))
    modulate(0)
    g2["out_r"][0].start()
    modulate(1)
    g2["out_l"][1].start()
    g2["out_r"][1].start()
    g2["out_l"][0].start()
    for c in range(PARTS):
        g2["own"][c].start()

    def mix(n, fresh=False):
        b = order[n]
        load_o[n].wait()
        part = jnp.dot(mod[b], wout[b], preferred_element_type=F32)
        if fresh:
            total[...] = part
        else:
            total[...] += part

    def mix_sibling():
        for c in range(PARTS):
            g2["own"][c].wait_recv()
        mix(1)

    def mix_near():
        mix(2)
        mix(3)

    def mix_near_other():
        mix(4)
        mix(5)

    def mix_last():
        b = order[7]
        load_o[7].wait()
        out[...] = (total[...] + jnp.dot(mod[b], wout[b], preferred_element_type=F32)).astype(BF16)

    relay(g2, lambda: mix(0, True), (mix_sibling, mix_near, mix_near_other), (lambda: mix(6), mix_last))

    finish(g1)
    finish(g2)

    @pl.when(ctx < CTX - 1)
    def _():
        tail.wait_send()

    for ahead in range(1, CTX):
        @pl.when(ctx + ahead < CTX)
        def _():
            pltpu.make_async_remote_copy(
                src_ref=state_out, dst_ref=state_in.at[ctx], send_sem=st_send.at[ahead], recv_sem=st_recv.at[ctx],
                device_id=(lax.rem(ctx + ahead, CTX), me), device_id_type=MESH).wait_send()


def per_device(tokens, w_in, short_kernel, residue, rate, w_out):
    w_in = jnp.transpose(w_in, (1, 0, 2)).reshape(3, BLOCKS, WIDE, WIDE)
    w_out = w_out.reshape(BLOCKS, WIDE, WIDE)
    vmem = pl.BlockSpec(memory_space=pltpu.VMEM)
    hbm = pl.BlockSpec(memory_space=pl.ANY)
    dma = pltpu.SemaphoreType.DMA
    return pl.pallas_call(
        kernel,
        out_shape=jax.ShapeDtypeStruct((ROWS, WIDE), BF16),
        in_specs=[hbm, hbm, vmem, vmem, vmem, hbm],
        out_specs=vmem,
        scratch_shapes=[
            pltpu.VMEM((3, BLOCKS, WIDE, WIDE), BF16),
            pltpu.VMEM((BLOCKS, WIDE, WIDE), BF16),
            pltpu.VMEM((BLOCKS, ROWS, WIDE), BF16),
            pltpu.VMEM((BLOCKS, ROWS, WIDE), BF16),
            pltpu.VMEM((3, PAD + ROWS, WIDE), F32),
            pltpu.VMEM((ROWS, WIDE), F32),
            pltpu.VMEM((TILES, ROWS + SUB, LANES), F32),
            pltpu.VMEM((TILES, ROWS + SUB, LANES), F32),
            pltpu.VMEM((TILES, ROWS, LANES), F32),
            pltpu.VMEM((6, MODES, WIDE), F32),
            pltpu.VMEM((MODES, WIDE), F32),
            pltpu.VMEM((MODES, 8, WIDE), F32),
            pltpu.VMEM((MODES, 8, WIDE), F32),
            pltpu.VMEM((8, WIDE), F32),
            pltpu.VMEM((8, WIDE), F32),
            pltpu.VMEM((MODES, WIDE), F32),
            pltpu.VMEM((CTX, MODES, WIDE), F32),
            dma((BLOCKS,)), dma((BLOCKS,)), dma,
            dma((16,)), dma((16,)), dma((16,)), dma((16,)),
            dma((1,)), dma((1,)), dma((CTX,)), dma((CTX,)),
        ],
        compiler_params=pltpu.CompilerParams(
            collective_id=0, has_side_effects=True, vmem_limit_bytes=48 * 2**20),
        cost_estimate=pl.CostEstimate(
            flops=2 * ROWS * 4096 * 2048, bytes_accessed=17 * 2**20, transcendentals=0),
    )(tokens, w_in, short_kernel, residue.T, rate.T, w_out)


def solution(mesh):
    in_specs = (
        P("ctx", "chan"),
        P(None, None, "chan"),
        P(None, None, "chan"),
        P("chan", None),
        P("chan", None),
        P(None, "chan"),
    )
    return jax.shard_map(
        per_device, mesh=mesh, in_specs=in_specs, out_specs=P("ctx", "chan"), check_vma=False)
```

```python
import jax
import jax.numpy as jnp
from jax import lax
from jax.experimental import pallas as pl
from jax.experimental.pallas import tpu as pltpu
from jax.sharding import PartitionSpec as P

MESH = pl.DeviceIdType.MESH
F32 = jnp.float32
BF16 = jnp.bfloat16
STATE = jnp.float32
CTX = 16
ROWS = 256
WIDE = 512
BLOCKS = 8
MODES = 16
SHORT = 3
RUNS = 8
SUB = ROWS // RUNS
LANES = 128
TILES = WIDE // LANES
HALF = WIDE // 2
TALL = ROWS // 2
HEAD = 16


def remote(src, dst, send, recv, where):
    return pltpu.make_async_remote_copy(
        src_ref=src, dst_ref=dst, send_sem=send, recv_sem=recv, device_id=where, device_id_type=MESH)


class Gather:
    def __init__(self, source, store, top, block, left, right, far, dev, send, recv):
        count = [0]

        def copy(src, dst, where):
            s = count[0]
            count[0] += 1
            return remote(src, dst, send.at[s], recv.at[s], where)

        def here(owner, c, h):
            return store.at[owner, pl.ds(top + h * TALL, TALL), pl.ds(c * HALF, HALF)]

        quarters = [(c, h) for c in range(2) for h in range(2)]
        to_right, to_left, to_other = dev(1), dev(3), dev(0, True)
        self.right = {q: copy(source(*q), here(block, *q), to_right) for q in quarters}
        self.left = {q: copy(source(*q), here(block, *q), to_left) for q in quarters}
        self.own = {q: copy(source(*q), here(block, *q), to_other) for q in quarters}
        self.on_right = [copy(here(left, c, 0), here(left, c, 0), to_right) for c in range(2)]
        self.on_left = [copy(here(right, c, 1), here(right, c, 1), to_left) for c in range(2)]
        self.side_l = {q: copy(here(left, *q), here(left, *q), to_other) for q in quarters}
        self.side_r = {q: copy(here(right, *q), here(right, *q), to_other) for q in quarters}
        self.side_f = {q: copy(here(far, *q), here(far, *q), to_other) for q in quarters}

    def begin(self, c):
        for h in range(2):
            self.right[c, h].start()
            self.left[c, 1 - h].start()
        for h in range(2):
            self.own[c, h].start()

    def relay(self, work):
        work[0]()
        for c in range(2):
            self.right[c, 0].wait_recv()
            self.on_right[c].start()
            self.side_l[c, 0].start()
            self.left[c, 1].wait_recv()
            self.on_left[c].start()
            self.side_r[c, 1].start()
            work[1 + 2 * c]()
            self.right[c, 1].wait_recv()
            self.side_l[c, 1].start()
            self.left[c, 0].wait_recv()
            self.side_r[c, 0].start()
            work[2 + 2 * c]()
        for c in range(2):
            self.on_right[c].wait_recv()
            self.side_f[c, 0].start()
            self.on_left[c].wait_recv()
            self.side_f[c, 1].start()
            work[5 + c]()

    def wait_side(self, sides, c):
        for side in sides:
            for h in range(2):
                side[c, h].wait_recv()

    def finish(self):
        for group in (self.right, self.left, self.own, self.side_l, self.side_r, self.side_f):
            for c in group.values():
                c.wait_send()
        for c in self.on_right + self.on_left:
            c.wait_send()


def total_of(terms):
    while len(terms) > 1:
        terms = [a + b for a, b in zip(terms[::2], terms[1::2])]
    return terms[0]


def kernel(tok, w_in, taps_hbm, residue_hbm, rate_hbm, w_out, out,
           taps, residue, rate, win, wout, gat, mod, acc, total, gated, conv, gate0,
           decay, weight, run_state, run_decay, ramp, halo_out, halo_in, state_out, state_in, entry,
           w_sems, o_sems, own_sem, small_sems, send1, recv1, send2, recv2, halo_send, halo_recv,
           state_send, state_recv, ready, next_in, later_in):
    me = lax.axis_index("chan")
    ctx = lax.axis_index("ctx")
    x, core = me // 2, me % 2

    def at(step, flip=False):
        return lax.rem(x + step, 4) * 2 + (1 - core if flip else core)

    def dev(step, flip=False):
        return (ctx, at(step, flip))

    order = [me, at(0, True), at(3), at(1), at(3, True), at(1, True), at(2), at(2, True)]

    load_w = [pltpu.make_async_copy(w_in.at[:, b], win.at[:, b], w_sems.at[n]) for n, b in enumerate(order)]
    load_o = [pltpu.make_async_copy(w_out.at[b], wout.at[b], o_sems.at[n]) for n, b in enumerate(order)]
    load_t = pltpu.make_async_copy(tok, gat.at[me, pl.ds(HEAD, ROWS)], own_sem)
    load_s = [pltpu.make_async_copy(src, dst, small_sems.at[n]) for n, (src, dst) in enumerate(
        ((rate_hbm, rate), (residue_hbm, residue), (taps_hbm, taps)))]

    barrier = pltpu.get_barrier_semaphore()

    def greet(sem, where):
        pl.semaphore_signal(sem, inc=1, device_id=where, device_id_type=MESH)

    def chip(step, of_core):
        return (ctx, lax.rem(x + step, 4) * 2 + of_core)

    load_t.start()
    for c in load_s:
        c.start()

    @pl.when(core == 0)
    def _():
        greet(barrier, chip(1, 0))
        greet(barrier, chip(3, 0))
        pl.semaphore_wait(barrier, 5)
        for step in (0, 1, 3):
            greet(ready, chip(step, 1))

    @pl.when(core == 1)
    def _():
        for step in (0, 1, 3):
            greet(barrier, chip(step, 0))
        pl.semaphore_wait(ready, 3)

    ring = (me, at(3), at(1), at(2), dev)
    g1 = Gather(lambda c, h: tok.at[pl.ds(h * TALL, TALL), pl.ds(c * HALF, HALF)], gat, HEAD, *ring, send1, recv1)
    g1.begin(0)
    g1.begin(1)

    even = lax.rem(x, 2) == 0

    @pl.when((core == 1) & even & (ctx > 0))
    def _():
        greet(barrier, (ctx - 1, me))

    for back in range(1, CTX):
        @pl.when((core == 1) & jnp.logical_not(even) & (ctx >= back))
        def _():
            greet(barrier, (ctx - back, me))

    load_w[0].start()
    load_w[1].start()
    load_t.wait()
    row16 = lax.broadcasted_iota(jnp.int32, (HEAD, LANES), 0)
    packed = jnp.zeros((HEAD, LANES), F32)
    for t in range(TILES):
        last = gat[me, ROWS:ROWS + HEAD, t * LANES:(t + 1) * LANES].astype(F32)
        packed = jnp.where(row16 // 2 == t, pltpu.roll(last, 2 * t + 2, 0), packed)
    halo_out[...] = packed.astype(BF16)
    halos = [remote(halo_out, halo_in.at[me], halo_send.at[o], halo_recv.at[me],
                    (lax.rem(ctx + 1, CTX), lax.rem(me + o, BLOCKS))) for o in range(BLOCKS)]

    for n in range(2, BLOCKS):
        load_w[n].start()
    for n in range(BLOCKS):
        load_o[n].start()
    for c in load_s:
        c.wait()

    decay[0] = jnp.exp(-rate[...])
    for n, power in enumerate((8, 32, 64, 128, 256)):
        decay[n + 1] = jnp.exp(-rate[...] * float(power))
    weight[...] = residue[...] * jnp.sqrt(1.0 - jnp.exp(-2.0 * rate[...]))
    sublane = lax.broadcasted_iota(jnp.int32, (8, WIDE), 0).astype(F32)
    for r in range(MODES):
        ramp[r] = jnp.exp(-rate[r:r + 1] * (sublane + 1.0)) * weight[r:r + 1]
        run_decay[r] = jnp.exp(-rate[r:r + 1] * (float(SUB) * (float(RUNS - 1) - sublane)))

    def project(n, part=None, fresh=False, slots=(0, 1, 2), last=False):
        b = order[n]
        cols = slice(0, WIDE) if part is None else slice(part * HALF, (part + 1) * HALF)
        for s in slots:
            value = jnp.dot(gat[b, :, cols], win[s, b, cols], preferred_element_type=F32)
            if not fresh:
                value = acc[s] + value
            if last:
                value = value.astype(BF16).astype(F32)
            acc[s] = value

    def take_halo():
        @pl.when(ctx > 0)
        def _():
            for q in range(BLOCKS):
                remote(halo_out, halo_in.at[q], halo_send.at[0], halo_recv.at[q], dev(1)).wait_recv()
                rows = halo_in[q].astype(F32)
                for t in range(TILES):
                    gat[q, 0:HEAD, t * LANES:(t + 1) * LANES] = pltpu.roll(rows, HEAD - 2 - 2 * t, 0).astype(BF16)

        @pl.when(ctx == 0)
        def _():
            for q in range(BLOCKS):
                gat[q, 0:HEAD] = jnp.zeros((HEAD, WIDE), BF16)

    def project_own():
        load_w[0].wait()
        project(0, fresh=True)

    def project_other():
        load_w[1].wait()
        for c in range(2):
            g1.wait_side([g1.own], c)
        project(1)

    def project_near():
        load_w[2].wait()
        project(2)
        load_w[3].wait()
        project(3)

    def project_near_other():
        for c in range(2):
            g1.wait_side([g1.side_l, g1.side_r], c)
        load_w[4].wait()
        project(4)

    def project_far():
        load_w[5].wait()
        project(5)
        load_w[6].wait()
        project(6, 0)
        load_w[7].wait()
        g1.wait_side([g1.side_f], 0)
        project(7, 0)
        project(6, 1)
        g1.wait_side([g1.side_f], 1)
        project(7, 1, slots=(1, 2), last=True)

    def hear_next():
        @pl.when((ctx < CTX - 1) & (core == 1) & even)
        def _():
            pl.semaphore_wait(barrier, 1)
            for where in (chip(0, 0), chip(1, 0), chip(1, 1)):
                greet(next_in, where)

    def send_halo():
        @pl.when((ctx < CTX - 1) & jnp.logical_not((core == 1) & even))
        def _():
            pl.semaphore_wait(next_in, 1)

        @pl.when(ctx < CTX - 1)
        def _():
            for c in halos:
                c.start()

    def hear_later():
        @pl.when((ctx < CTX - 1) & (core == 1) & jnp.logical_not(even))
        def _():
            pl.semaphore_wait(barrier, CTX - 1 - ctx)
            for where in (chip(0, 0), chip(3, 0), chip(3, 1)):
                greet(later_in, where)

    def idle():
        pass

    def project_first():
        take_halo()
        project_own()
        project_other()

    def project_middle():
        hear_later()
        project_near()
        project_near_other()

    g1.relay((hear_next, send_halo, idle, idle, project_first, project_middle, project_far))

    def filtered(s, q, lanes):
        value = None
        for tap in range(SHORT):
            first = HEAD + SUB * q - tap
            term = taps[tap, s:s + 1, lanes] * acc[s, first:first + SUB, lanes]
            value = term if value is None else value + term
        return value

    row = lax.broadcasted_iota(jnp.int32, (8, LANES), 0)

    def spread(ref, r, lanes):
        return jnp.broadcast_to(ref[r:r + 1, lanes], (8, LANES))

    def lanes_of(tile):
        return pl.ds(pl.multiple_of(tile * LANES, LANES), LANES)

    def block_state(half):
        for t in range(2 * half, 2 * half + 2):
            lanes = slice(t * LANES, (t + 1) * LANES)
            for q in range(RUNS):
                gated[t, SUB * q:SUB * (q + 1)] = (
                    filtered(1, q, lanes) * filtered(2, q, lanes)).astype(BF16).astype(F32)

        @pl.loop(2 * half, 2 * half + 2)
        def _(tile):
            lanes = lanes_of(tile)
            d = [spread(decay.at[0], r, lanes) for r in range(MODES)]

            def step(j, states):
                g = gated[tile, pl.ds(j, RUNS, stride=SUB)]
                return tuple(d[r] * states[r] + g for r in range(MODES))

            states = lax.fori_loop(0, SUB, step, tuple(jnp.zeros((8, LANES), F32) for _ in range(MODES)), unroll=8)
            where = pl.ds(pl.multiple_of((tile - 2 * half) * LANES, LANES), LANES)
            for r in range(MODES):
                run_state[r, :, lanes] = states[r]
                state_out[half, r:r + 1, where] = jnp.sum(
                    run_decay[r, :, lanes] * states[r], axis=0, keepdims=True).astype(STATE)

        if half == 0:
            @pl.when((ctx < CTX - 1) & jnp.logical_not((core == 1) & jnp.logical_not(even)))
            def _():
                pl.semaphore_wait(later_in, 1)

        for ahead in range(1, CTX):
            @pl.when(ctx + ahead < CTX)
            def _():
                remote(state_out.at[half], state_in.at[half, ctx], state_send.at[half, ahead], state_recv.at[half, ctx],
                       (lax.rem(ctx + ahead, CTX), me)).start()

    block_state(0)
    block_state(1)
    project(7, 1, slots=(0,), last=True)

    def own_part(half):
        for t in range(2 * half, 2 * half + 2):
            lanes = slice(t * LANES, (t + 1) * LANES)
            for q in range(RUNS):
                gate0[t, SUB * q:SUB * (q + 1)] = filtered(0, q, lanes)

        @pl.loop(2 * half, 2 * half + 2)
        def _(tile):
            lanes = lanes_of(tile)
            before = []
            for r in range(MODES):
                s = run_state[r, :, lanes]
                for n, shift in enumerate((1, 2, 4)):
                    s = s + jnp.where(row >= shift, spread(decay.at[2 + n], r, lanes) * pltpu.roll(s, shift, 0), 0.0)
                before.append(jnp.where(row >= 1, pltpu.roll(s, 1, 0), 0.0))
            d = [spread(decay.at[0], r, lanes) for r in range(MODES)]
            w = [spread(weight, r, lanes) for r in range(MODES)]

            def step(j, states):
                g = gated[tile, pl.ds(j, RUNS, stride=SUB)]
                sums = [None] * 4
                after = []
                for r in range(MODES):
                    s = d[r] * states[r] + g
                    after.append(s)
                    term = w[r] * s
                    sums[r % 4] = term if sums[r % 4] is None else sums[r % 4] + term
                conv[tile, pl.ds(j, RUNS, stride=SUB)] = total_of(sums)
                return tuple(after)

            lax.fori_loop(0, SUB, step, tuple(before), unroll=2)

    own_part(0)
    own_part(1)

    def merge(half):
        def add(j, value):
            remote(state_out.at[half], state_in.at[half, j], state_send.at[half, 0], state_recv.at[half, j],
                   dev(1)).wait_recv()
            return decay[5, :, half * HALF:(half + 1) * HALF] * value + state_in[half, j].astype(F32)

        entry[:, half * HALF:(half + 1) * HALF] = lax.fori_loop(0, ctx, add, jnp.zeros((MODES, HALF), F32))

    def modulate(half):
        @pl.loop(2 * half, 2 * half + 2)
        def _(tile):
            lanes = lanes_of(tile)
            z = tuple(ramp[r, :, lanes] * entry[r:r + 1, lanes] for r in range(MODES))
            d8 = [spread(decay.at[1], r, lanes) for r in range(MODES)]

            def step(q, z):
                halves = []
                for part in range(2):
                    rows = pl.ds(pl.multiple_of(q * 16 + part * 8, 8), 8)
                    halves.append(gate0[tile, rows] * (conv[tile, rows] + total_of(list(z))))
                    z = tuple(d8[r] * z[r] for r in range(MODES))
                mod[me, pl.ds(pl.multiple_of(q * 16, 16), 16), lanes] = jnp.concatenate(halves, 0).astype(BF16)
                return z

            lax.fori_loop(0, ROWS // 16, step, z, unroll=2)

    g2 = Gather(lambda c, h: mod.at[me, pl.ds(h * TALL, TALL), pl.ds(c * HALF, HALF)], mod, 0, *ring, send2, recv2)
    for half in range(2):
        merge(half)
        modulate(half)
        g2.begin(half)

    def mix(n, part=None, fresh=False):
        b = order[n]
        cols = slice(0, WIDE) if part is None else slice(part * HALF, (part + 1) * HALF)
        value = jnp.dot(mod[b, :, cols], wout[b, cols], preferred_element_type=F32)
        total[...] = value if fresh else total[...] + value

    def mix_own():
        for c in load_o:
            c.wait()
        mix(0, fresh=True)

    def mix_other():
        for c in range(2):
            g2.wait_side([g2.own], c)
        mix(1)

    def mix_near():
        mix(2)
        mix(3)

    def mix_near_other():
        for c in range(2):
            g2.wait_side([g2.side_l, g2.side_r], c)
        mix(4)
        mix(5)
        mix(6, 0)

    def mix_far():
        g2.wait_side([g2.side_f], 0)
        mix(7, 0)
        mix(6, 1)
        g2.wait_side([g2.side_f], 1)
        b = order[7]
        out[...] = (total[...] + jnp.dot(
            mod[b, :, HALF:], wout[b, HALF:], preferred_element_type=F32)).astype(BF16)

    g2.relay((idle, mix_own, mix_other, idle, mix_near, mix_near_other, mix_far))

    g1.finish()
    g2.finish()

    @pl.when(ctx < CTX - 1)
    def _():
        for c in halos:
            c.wait_send()

    for half in range(2):
        for ahead in range(1, CTX):
            @pl.when(ctx + ahead < CTX)
            def _():
                remote(state_out.at[half], state_in.at[half, ctx], state_send.at[half, ahead],
                       state_recv.at[half, ctx], (lax.rem(ctx + ahead, CTX), me)).wait_send()


def per_device(tokens, w_in, short_kernel, residue, rate, w_out):
    w_in = jnp.transpose(w_in, (1, 0, 2)).reshape(3, BLOCKS, WIDE, WIDE)
    w_out = w_out.reshape(BLOCKS, WIDE, WIDE)
    dma = pltpu.SemaphoreType.DMA
    vmem = pltpu.VMEM
    return pl.pallas_call(
        kernel,
        out_shape=jax.ShapeDtypeStruct((ROWS, WIDE), BF16),
        in_specs=[pl.BlockSpec(memory_space=pltpu.HBM)] * 6,
        out_specs=pl.BlockSpec(memory_space=pltpu.VMEM),
        scratch_shapes=[
            vmem((SHORT, 3, WIDE), F32),
            vmem((MODES, WIDE), F32),
            vmem((MODES, WIDE), F32),
            vmem((3, BLOCKS, WIDE, WIDE), BF16),
            vmem((BLOCKS, WIDE, WIDE), BF16),
            vmem((BLOCKS, HEAD + ROWS, WIDE), BF16),
            vmem((BLOCKS, ROWS, WIDE), BF16),
            vmem((3, HEAD + ROWS, WIDE), F32),
            vmem((ROWS, WIDE), F32),
            vmem((TILES, ROWS + SUB, LANES), F32),
            vmem((TILES, ROWS + SUB, LANES), F32),
            vmem((TILES, ROWS, LANES), F32),
            vmem((6, MODES, WIDE), F32),
            vmem((MODES, WIDE), F32),
            vmem((MODES, 8, WIDE), F32),
            vmem((MODES, 8, WIDE), F32),
            vmem((MODES, 8, WIDE), F32),
            vmem((HEAD, LANES), BF16),
            vmem((BLOCKS, HEAD, LANES), BF16),
            vmem((2, MODES, HALF), STATE),
            vmem((2, CTX, MODES, HALF), STATE),
            vmem((MODES, WIDE), F32),
            dma((BLOCKS,)), dma((BLOCKS,)), dma, dma((3,)),
            dma((32,)), dma((32,)), dma((32,)), dma((32,)),
            dma((BLOCKS,)), dma((BLOCKS,)),
            dma((2, CTX)), dma((2, CTX)),
            pltpu.SemaphoreType.REGULAR, pltpu.SemaphoreType.REGULAR, pltpu.SemaphoreType.REGULAR,
        ],
        compiler_params=pltpu.CompilerParams(
            collective_id=0, has_side_effects=True, vmem_limit_bytes=60 * 2**20),
        cost_estimate=pl.CostEstimate(
            flops=2 * ROWS * 4096 * 2048, bytes_accessed=17 * 2**20, transcendentals=0),
    )(tokens, w_in, short_kernel, residue.T, rate.T, w_out)


def solution(mesh):
    in_specs = (
        P("ctx", "chan"),
        P(None, None, "chan"),
        P(None, None, "chan"),
        P("chan", None),
        P("chan", None),
        P(None, "chan"),
    )
    return jax.shard_map(
        per_device, mesh=mesh, in_specs=in_specs, out_specs=P("ctx", "chan"), check_vma=False)
```

```python
import jax
import jax.numpy as jnp
from jax import lax
from jax.experimental import pallas as pl
from jax.experimental.pallas import tpu as pltpu
from jax.sharding import PartitionSpec as P

MESH = pl.DeviceIdType.MESH
F32 = jnp.float32
BF16 = jnp.bfloat16
STATE = jnp.bfloat16
CTX = 16
ROWS = 256
WIDE = 512
BLOCKS = 8
MODES = 16
SHORT = 3
RUNS = 8
SUB = ROWS // RUNS
LANES = 128
TILES = WIDE // LANES
HALF = WIDE // 2
TALL = ROWS // 2
HEAD = 16


def remote(src, dst, send, recv, where):
    return pltpu.make_async_remote_copy(
        src_ref=src, dst_ref=dst, send_sem=send, recv_sem=recv, device_id=where, device_id_type=MESH)


class Gather:
    def __init__(self, source, store, top, block, left, right, far, dev, send, recv):
        count = [0]

        def copy(src, dst, where):
            s = count[0]
            count[0] += 1
            return remote(src, dst, send.at[s], recv.at[s], where)

        def here(owner, c, h):
            return store.at[owner, pl.ds(top + h * TALL, TALL), pl.ds(c * HALF, HALF)]

        quarters = [(c, h) for c in range(2) for h in range(2)]
        to_right, to_left, to_other = dev(1), dev(3), dev(0, True)
        self.right = {q: copy(source(*q), here(block, *q), to_right) for q in quarters}
        self.left = {q: copy(source(*q), here(block, *q), to_left) for q in quarters}
        self.own = {q: copy(source(*q), here(block, *q), to_other) for q in quarters}
        self.on_right = [copy(here(left, c, 0), here(left, c, 0), to_right) for c in range(2)]
        self.on_left = [copy(here(right, c, 1), here(right, c, 1), to_left) for c in range(2)]
        self.side_l = {q: copy(here(left, *q), here(left, *q), to_other) for q in quarters}
        self.side_r = {q: copy(here(right, *q), here(right, *q), to_other) for q in quarters}
        self.side_f = {q: copy(here(far, *q), here(far, *q), to_other) for q in quarters}

    def begin(self, c):
        for h in range(2):
            self.right[c, h].start()
            self.left[c, 1 - h].start()
        for h in range(2):
            self.own[c, h].start()

    def relay(self, work):
        work[0]()
        for c in range(2):
            self.right[c, 0].wait_recv()
            self.on_right[c].start()
            self.side_l[c, 0].start()
            self.left[c, 1].wait_recv()
            self.on_left[c].start()
            self.side_r[c, 1].start()
            work[1 + 2 * c]()
            self.right[c, 1].wait_recv()
            self.side_l[c, 1].start()
            self.left[c, 0].wait_recv()
            self.side_r[c, 0].start()
            work[2 + 2 * c]()
        for c in range(2):
            self.on_right[c].wait_recv()
            self.side_f[c, 0].start()
            self.on_left[c].wait_recv()
            self.side_f[c, 1].start()
            work[5 + c]()

    def wait_side(self, sides, c):
        for side in sides:
            for h in range(2):
                side[c, h].wait_recv()

    def finish(self, late=None):
        early = [self.right, self.left, self.own, self.side_l, self.side_r]
        if late is not True:
            for group in early:
                for c in group.values():
                    c.wait_send()
        if late is not False:
            for c in list(self.side_f.values()) + self.on_right + self.on_left:
                c.wait_send()


def total_of(terms):
    while len(terms) > 1:
        terms = [a + b for a, b in zip(terms[::2], terms[1::2])]
    return terms[0]


def kernel(tok, w_in, taps_hbm, residue_hbm, rate_hbm, w_out, out,
           taps, residue, rate, win, wout, gat, mod, acc, total, gated, conv, gate0,
           decay, weight, run_state, run_decay, ramp, halo_out, halo_in, state_out, state_in, entry,
           w_sems, o_sems, own_sem, small_sems, send1, recv1, send2, recv2, halo_send, halo_recv,
           state_send, state_recv, ready, next_in, later_in):
    me = lax.axis_index("chan")
    ctx = lax.axis_index("ctx")
    x, core = me // 2, me % 2

    def at(step, flip=False):
        return lax.rem(x + step, 4) * 2 + (1 - core if flip else core)

    def dev(step, flip=False):
        return (ctx, at(step, flip))

    order = [me, at(0, True), at(3), at(1), at(3, True), at(1, True), at(2), at(2, True)]

    load_w = [pltpu.make_async_copy(w_in.at[:, b], win.at[:, b], w_sems.at[n]) for n, b in enumerate(order)]
    load_o = [pltpu.make_async_copy(w_out.at[b], wout.at[b], o_sems.at[n]) for n, b in enumerate(order)]
    load_t = pltpu.make_async_copy(tok, gat.at[me, pl.ds(HEAD, ROWS)], own_sem)
    load_s = [pltpu.make_async_copy(src, dst, small_sems.at[n]) for n, (src, dst) in enumerate(
        ((rate_hbm, rate), (residue_hbm, residue), (taps_hbm, taps)))]

    barrier = pltpu.get_barrier_semaphore()

    def greet(sem, where):
        pl.semaphore_signal(sem, inc=1, device_id=where, device_id_type=MESH)

    def chip(step, of_core):
        return (ctx, lax.rem(x + step, 4) * 2 + of_core)

    load_t.start()
    for c in load_s:
        c.start()

    @pl.when(core == 0)
    def _():
        greet(barrier, chip(1, 0))
        greet(barrier, chip(3, 0))
        pl.semaphore_wait(barrier, 5)
        for step in (0, 1, 3):
            greet(ready, chip(step, 1))

    @pl.when(core == 1)
    def _():
        for step in (0, 1, 3):
            greet(barrier, chip(step, 0))
        pl.semaphore_wait(ready, 3)

    ring = (me, at(3), at(1), at(2), dev)
    g1 = Gather(lambda c, h: tok.at[pl.ds(h * TALL, TALL), pl.ds(c * HALF, HALF)], gat, HEAD, *ring, send1, recv1)
    g1.begin(0)
    g1.begin(1)

    even = lax.rem(x, 2) == 0

    @pl.when((core == 1) & even & (ctx > 0))
    def _():
        greet(barrier, (ctx - 1, me))

    for back in range(1, CTX):
        @pl.when((core == 1) & jnp.logical_not(even) & (ctx >= back))
        def _():
            greet(barrier, (ctx - back, me))

    load_w[0].start()
    load_w[1].start()
    load_t.wait()
    row16 = lax.broadcasted_iota(jnp.int32, (HEAD, LANES), 0)
    packed = jnp.zeros((HEAD, LANES), F32)
    for t in range(TILES):
        last = gat[me, ROWS:ROWS + HEAD, t * LANES:(t + 1) * LANES].astype(F32)
        packed = jnp.where(row16 // 2 == t, pltpu.roll(last, 2 * t + 2, 0), packed)
    halo_out[...] = packed.astype(BF16)
    halos = [remote(halo_out, halo_in.at[me], halo_send.at[o], halo_recv.at[me],
                    (lax.rem(ctx + 1, CTX), lax.rem(me + o, BLOCKS))) for o in range(BLOCKS)]

    for n in range(2, BLOCKS):
        load_w[n].start()
    for n in range(BLOCKS):
        load_o[n].start()
    @pl.when((ctx < CTX - 1) & (core == 1) & even)
    def _():
        pl.semaphore_wait(barrier, 1)
        for where in (chip(0, 0), chip(1, 0), chip(1, 1)):
            greet(next_in, where)

    @pl.when((ctx < CTX - 1) & jnp.logical_not((core == 1) & even))
    def _():
        pl.semaphore_wait(next_in, 1)

    @pl.when(ctx < CTX - 1)
    def _():
        for c in halos:
            c.start()

    for c in load_s:
        c.wait()

    decay[0] = jnp.exp(-rate[...])
    for n, power in enumerate((8, 32, 64, 128, 256)):
        decay[n + 1] = jnp.exp(-rate[...] * float(power))
    weight[...] = residue[...] * jnp.sqrt(1.0 - jnp.exp(-2.0 * rate[...]))
    sublane = lax.broadcasted_iota(jnp.int32, (8, WIDE), 0).astype(F32)
    for r in range(MODES):
        ramp[r] = jnp.exp(-rate[r:r + 1] * (sublane + 1.0)) * weight[r:r + 1]
        run_decay[r] = jnp.exp(-rate[r:r + 1] * (float(SUB) * (float(RUNS - 1) - sublane)))

    ALL, BODY, TOP = slice(0, HEAD + ROWS), slice(HEAD, HEAD + ROWS), slice(0, HEAD)

    def project(n, part=None, rows=ALL, fresh=False, slots=(0, 1, 2), last=False):
        b = order[n]
        cols = slice(0, WIDE) if part is None else slice(part * HALF, (part + 1) * HALF)
        for s in slots:
            value = jnp.dot(gat[b, rows, cols], win[s, b, cols], preferred_element_type=F32)
            if not fresh:
                value = acc[s, rows] + value
            if last:
                value = value.astype(BF16).astype(F32)
            acc[s, rows] = value

    def take_halo():
        @pl.when(ctx > 0)
        def _():
            for q in range(BLOCKS):
                remote(halo_out, halo_in.at[q], halo_send.at[0], halo_recv.at[q], dev(1)).wait_recv()
                rows = halo_in[q].astype(F32)
                for t in range(TILES):
                    gat[q, 0:HEAD, t * LANES:(t + 1) * LANES] = pltpu.roll(rows, HEAD - 2 - 2 * t, 0).astype(BF16)

        @pl.when(ctx == 0)
        def _():
            for q in range(BLOCKS):
                gat[q, 0:HEAD] = jnp.zeros((HEAD, WIDE), BF16)

    def project_own():
        load_w[0].wait()
        project(0, rows=BODY, fresh=True)

    def project_other():
        load_w[1].wait()
        for c in range(2):
            g1.wait_side([g1.own], c)
        project(1, rows=BODY)

    def project_near():
        load_w[2].wait()
        project(2, rows=BODY)
        load_w[3].wait()
        project(3, rows=BODY)

    def project_near_other():
        hear_later()
        take_halo()
        for c in range(2):
            g1.wait_side([g1.side_l, g1.side_r], c)
        project(0, rows=TOP, fresh=True)
        project(1, rows=TOP)
        load_w[4].wait()
        project(4)

    def project_far():
        load_w[5].wait()
        project(5)
        project(2, rows=TOP)
        project(3, rows=TOP)
        load_w[6].wait()
        project(6)
        load_w[7].wait()
        g1.wait_side([g1.side_f], 0)
        project(7, 0)
        g1.wait_side([g1.side_f], 1)
        project(7, 1, slots=(1, 2), last=True)

    def hear_later():
        @pl.when((ctx < CTX - 1) & (core == 1) & jnp.logical_not(even))
        def _():
            pl.semaphore_wait(barrier, CTX - 1 - ctx)
            for where in (chip(0, 0), chip(3, 0), chip(3, 1)):
                greet(later_in, where)

    def idle():
        pass

    g1.relay((idle, project_own, project_other, idle, project_near, project_near_other, project_far))

    def filtered(s, q, lanes):
        value = None
        for tap in range(SHORT):
            first = HEAD + SUB * q - tap
            term = taps[tap, s:s + 1, lanes] * acc[s, first:first + SUB, lanes]
            value = term if value is None else value + term
        return value

    row = lax.broadcasted_iota(jnp.int32, (8, LANES), 0)

    def spread(ref, r, lanes):
        return jnp.broadcast_to(ref[r:r + 1, lanes], (8, LANES))

    def lanes_of(tile):
        return pl.ds(pl.multiple_of(tile * LANES, LANES), LANES)

    def block_state(half):
        for t in range(2 * half, 2 * half + 2):
            lanes = slice(t * LANES, (t + 1) * LANES)
            for q in range(RUNS):
                gated[t, SUB * q:SUB * (q + 1)] = (
                    filtered(1, q, lanes) * filtered(2, q, lanes)).astype(BF16).astype(F32)

        @pl.loop(2 * half, 2 * half + 2)
        def _(tile):
            lanes = lanes_of(tile)
            d = [spread(decay.at[0], r, lanes) for r in range(MODES)]

            def step(j, states):
                g = gated[tile, pl.ds(j, RUNS, stride=SUB)]
                return tuple(d[r] * states[r] + g for r in range(MODES))

            states = lax.fori_loop(0, SUB, step, tuple(jnp.zeros((8, LANES), F32) for _ in range(MODES)), unroll=8)
            where = pl.ds(pl.multiple_of((tile - 2 * half) * LANES, LANES), LANES)
            for r in range(MODES):
                run_state[r, :, lanes] = states[r]
                state_out[half, r:r + 1, where] = jnp.sum(
                    run_decay[r, :, lanes] * states[r], axis=0, keepdims=True).astype(STATE)

        if half == 0:
            @pl.when((ctx < CTX - 1) & jnp.logical_not((core == 1) & jnp.logical_not(even)))
            def _():
                pl.semaphore_wait(later_in, 1)

        for ahead in range(1, CTX):
            @pl.when(ctx + ahead < CTX)
            def _():
                remote(state_out.at[half], state_in.at[half, ctx], state_send.at[half, ahead], state_recv.at[half, ctx],
                       (lax.rem(ctx + ahead, CTX), me)).start()

    block_state(0)
    block_state(1)
    project(7, 1, slots=(0,), last=True)

    def own_part(half):
        for t in range(2 * half, 2 * half + 2):
            lanes = slice(t * LANES, (t + 1) * LANES)
            for q in range(RUNS):
                gate0[t, SUB * q:SUB * (q + 1)] = filtered(0, q, lanes)

        @pl.loop(2 * half, 2 * half + 2)
        def _(tile):
            lanes = lanes_of(tile)
            before = []
            for r in range(MODES):
                s = run_state[r, :, lanes]
                for n, shift in enumerate((1, 2, 4)):
                    s = s + jnp.where(row >= shift, spread(decay.at[2 + n], r, lanes) * pltpu.roll(s, shift, 0), 0.0)
                before.append(jnp.where(row >= 1, pltpu.roll(s, 1, 0), 0.0))
            d = [spread(decay.at[0], r, lanes) for r in range(MODES)]
            w = [spread(weight, r, lanes) for r in range(MODES)]

            def step(j, states):
                g = gated[tile, pl.ds(j, RUNS, stride=SUB)]
                sums = [None] * 4
                after = []
                for r in range(MODES):
                    s = d[r] * states[r] + g
                    after.append(s)
                    term = w[r] * s
                    sums[r % 4] = term if sums[r % 4] is None else sums[r % 4] + term
                conv[tile, pl.ds(j, RUNS, stride=SUB)] = total_of(sums)
                return tuple(after)

            lax.fori_loop(0, SUB, step, tuple(before), unroll=2)

    def merge(half):
        def add(j, value):
            remote(state_out.at[half], state_in.at[half, j], state_send.at[half, 0], state_recv.at[half, j],
                   dev(1)).wait_recv()
            return decay[5, :, half * HALF:(half + 1) * HALF] * value + state_in[half, j].astype(F32)

        entry[:, half * HALF:(half + 1) * HALF] = lax.fori_loop(0, ctx, add, jnp.zeros((MODES, HALF), F32))

    def modulate(half):
        @pl.loop(2 * half, 2 * half + 2)
        def _(tile):
            lanes = lanes_of(tile)
            z = tuple(ramp[r, :, lanes] * entry[r:r + 1, lanes] for r in range(MODES))
            d8 = [spread(decay.at[1], r, lanes) for r in range(MODES)]

            def step(q, z):
                halves = []
                for part in range(2):
                    rows = pl.ds(pl.multiple_of(q * 16 + part * 8, 8), 8)
                    halves.append(gate0[tile, rows] * (conv[tile, rows] + total_of(list(z))))
                    z = tuple(d8[r] * z[r] for r in range(MODES))
                mod[me, pl.ds(pl.multiple_of(q * 16, 16), 16), lanes] = jnp.concatenate(halves, 0).astype(BF16)
                return z

            lax.fori_loop(0, ROWS // 16, step, z, unroll=2)

    g2 = Gather(lambda c, h: mod.at[me, pl.ds(h * TALL, TALL), pl.ds(c * HALF, HALF)], mod, 0, *ring, send2, recv2)
    for half in range(2):
        own_part(half)
        merge(half)
        modulate(half)
        g2.begin(half)

    def mix(n, part=None, fresh=False):
        b = order[n]
        cols = slice(0, WIDE) if part is None else slice(part * HALF, (part + 1) * HALF)
        value = jnp.dot(mod[b, :, cols], wout[b, cols], preferred_element_type=F32)
        total[...] = value if fresh else total[...] + value

    def settle():
        g1.finish()

        @pl.when(ctx < CTX - 1)
        def _():
            for c in halos:
                c.wait_send()

        for half in range(2):
            for ahead in range(1, CTX):
                @pl.when(ctx + ahead < CTX)
                def _():
                    remote(state_out.at[half], state_in.at[half, ctx], state_send.at[half, ahead],
                           state_recv.at[half, ctx], (lax.rem(ctx + ahead, CTX), me)).wait_send()

    def mix_own():
        for c in load_o:
            c.wait()
        mix(0, fresh=True)

    def mix_other():
        for c in range(2):
            g2.wait_side([g2.own], c)
        mix(1)

    def mix_near():
        mix(2)
        mix(3)

    def mix_near_other():
        for c in range(2):
            g2.wait_side([g2.side_l, g2.side_r], c)
        mix(4)
        mix(5)
        mix(6, 0)
        g2.finish(late=False)

    def mix_far():
        g2.wait_side([g2.side_f], 0)
        mix(7, 0)
        mix(6, 1)
        g2.wait_side([g2.side_f], 1)
        b = order[7]
        out[...] = (total[...] + jnp.dot(
            mod[b, :, HALF:], wout[b, HALF:], preferred_element_type=F32)).astype(BF16)

    g2.relay((settle, mix_own, mix_other, idle, mix_near, mix_near_other, mix_far))

    g2.finish(late=True)


def per_device(tokens, w_in, short_kernel, residue, rate, w_out):
    w_in = jnp.transpose(w_in, (1, 0, 2)).reshape(3, BLOCKS, WIDE, WIDE)
    w_out = w_out.reshape(BLOCKS, WIDE, WIDE)
    dma = pltpu.SemaphoreType.DMA
    vmem = pltpu.VMEM
    return pl.pallas_call(
        kernel,
        out_shape=pltpu.VMEM((ROWS, WIDE), BF16),
        in_specs=[pl.BlockSpec(memory_space=pltpu.HBM)] * 6,
        out_specs=pl.BlockSpec(memory_space=pltpu.VMEM),
        scratch_shapes=[
            vmem((SHORT, 3, WIDE), F32),
            vmem((MODES, WIDE), F32),
            vmem((MODES, WIDE), F32),
            vmem((3, BLOCKS, WIDE, WIDE), BF16),
            vmem((BLOCKS, WIDE, WIDE), BF16),
            vmem((BLOCKS, HEAD + ROWS, WIDE), BF16),
            vmem((BLOCKS, ROWS, WIDE), BF16),
            vmem((3, HEAD + ROWS, WIDE), F32),
            vmem((ROWS, WIDE), F32),
            vmem((TILES, ROWS + SUB, LANES), F32),
            vmem((TILES, ROWS + SUB, LANES), F32),
            vmem((TILES, ROWS, LANES), F32),
            vmem((6, MODES, WIDE), F32),
            vmem((MODES, WIDE), F32),
            vmem((MODES, 8, WIDE), F32),
            vmem((MODES, 8, WIDE), F32),
            vmem((MODES, 8, WIDE), F32),
            vmem((HEAD, LANES), BF16),
            vmem((BLOCKS, HEAD, LANES), BF16),
            vmem((2, MODES, HALF), STATE),
            vmem((2, CTX, MODES, HALF), STATE),
            vmem((MODES, WIDE), F32),
            dma((BLOCKS,)), dma((BLOCKS,)), dma, dma((3,)),
            dma((32,)), dma((32,)), dma((32,)), dma((32,)),
            dma((BLOCKS,)), dma((BLOCKS,)),
            dma((2, CTX)), dma((2, CTX)),
            pltpu.SemaphoreType.REGULAR, pltpu.SemaphoreType.REGULAR, pltpu.SemaphoreType.REGULAR,
        ],
        compiler_params=pltpu.CompilerParams(
            collective_id=0, has_side_effects=True, vmem_limit_bytes=60 * 2**20),
        cost_estimate=pl.CostEstimate(
            flops=2 * ROWS * 4096 * 2048, bytes_accessed=17 * 2**20, transcendentals=0),
    )(tokens, w_in, short_kernel, residue.T, rate.T, w_out)


def solution(mesh):
    in_specs = (
        P("ctx", "chan"),
        P(None, None, "chan"),
        P(None, None, "chan"),
        P("chan", None),
        P("chan", None),
        P(None, "chan"),
    )
    return jax.shard_map(
        per_device, mesh=mesh, in_specs=in_specs, out_specs=P("ctx", "chan"), check_vma=False)
```

```python
import jax
import jax.numpy as jnp
from jax import lax
from jax.experimental import pallas as pl
from jax.experimental.pallas import tpu as pltpu
from jax.sharding import PartitionSpec as P

MESH = pl.DeviceIdType.MESH
F32 = jnp.float32
BF16 = jnp.bfloat16
STATE = jnp.bfloat16
CTX = 16
ROWS = 256
WIDE = 512
BLOCKS = 8
MODES = 16
SHORT = 3
RUNS = 8
SUB = ROWS // RUNS
LANES = 128
TILES = WIDE // LANES
HALF = WIDE // 2
TALL = ROWS // 2
HEAD = 16
SPLIT = (0, 2, TILES)


def remote(src, dst, send, recv, where):
    return pltpu.make_async_remote_copy(
        src_ref=src, dst_ref=dst, send_sem=send, recv_sem=recv, device_id=where, device_id_type=MESH)


class Gather:
    def __init__(self, source, here, block, left, right, far, dev, send, recv):
        count = [0]

        def copy(src, dst, where):
            s = count[0]
            count[0] += 1
            return remote(src, dst, send.at[s], recv.at[s], where)

        quarters = [(c, h) for c in range(2) for h in range(2)]
        to_right, to_left, to_other = dev(1), dev(3), dev(0, True)
        self.right = {q: copy(source(*q), here(block, *q), to_right) for q in quarters}
        self.left = {q: copy(source(*q), here(block, *q), to_left) for q in quarters}
        self.own = {q: copy(source(*q), here(block, *q), to_other) for q in quarters}
        self.on_right = [copy(here(left, c, 0), here(left, c, 0), to_right) for c in range(2)]
        self.on_left = [copy(here(right, c, 1), here(right, c, 1), to_left) for c in range(2)]
        self.side_l = {q: copy(here(left, *q), here(left, *q), to_other) for q in quarters}
        self.side_r = {q: copy(here(right, *q), here(right, *q), to_other) for q in quarters}
        self.side_f = {q: copy(here(far, *q), here(far, *q), to_other) for q in quarters}

    def begin(self, c):
        for h in range(2):
            self.right[c, h].start()
            self.left[c, 1 - h].start()
        for h in range(2):
            self.own[c, h].start()

    def begin_rows(self, c, h):
        self.right[c, h].start()
        if h == 1:
            self.left[c, 1].start()
            self.left[c, 0].start()
        self.own[c, h].start()

    def relay(self, work):
        work[0]()
        for c in range(2):
            self.right[c, 0].wait_recv()
            self.on_right[c].start()
            self.side_l[c, 0].start()
            self.left[c, 1].wait_recv()
            self.on_left[c].start()
            self.side_r[c, 1].start()
            work[1 + 2 * c]()
            self.right[c, 1].wait_recv()
            self.side_l[c, 1].start()
            self.left[c, 0].wait_recv()
            self.side_r[c, 0].start()
            work[2 + 2 * c]()
        for c in range(2):
            self.on_right[c].wait_recv()
            self.side_f[c, 0].start()
            self.on_left[c].wait_recv()
            self.side_f[c, 1].start()
            work[5 + c]()

    def wait_side(self, sides, c):
        for side in sides:
            for h in range(2):
                side[c, h].wait_recv()

    def finish(self, late=None):
        early = [self.right, self.left, self.own, self.side_l, self.side_r]
        if late is not True:
            for group in early:
                for c in group.values():
                    c.wait_send()
        if late is not False:
            for c in list(self.side_f.values()) + self.on_right + self.on_left:
                c.wait_send()


def total_of(terms):
    while len(terms) > 1:
        terms = [a + b for a, b in zip(terms[::2], terms[1::2])]
    return terms[0]


def kernel(tok, w_in, taps_hbm, residue_hbm, rate_hbm, w_out, out,
           taps, residue, rate, win, wout, gat, mod, acc, total, gated, conv, gate0,
           decay, weight, run_state, run_decay, ramp, halo_out, halo_in, state_out0, state_out1, state_in0, state_in1, entry,
           w_sems, o_sems, own_sem, small_sems, send1, recv1, send2, recv2, halo_send, halo_recv,
           state_send, state_recv, ready, ring_in, next_in, later_in):
    state_out, state_in = (state_out0, state_out1), (state_in0, state_in1)
    me = lax.axis_index("chan")
    ctx = lax.axis_index("ctx")
    x, core = me // 2, me % 2

    def at(step, flip=False):
        return lax.rem(x + step, 4) * 2 + (1 - core if flip else core)

    def dev(step, flip=False):
        return (ctx, at(step, flip))

    order = [me, at(0, True), at(3), at(1), at(3, True), at(1, True), at(2), at(2, True)]

    load_w = [pltpu.make_async_copy(w_in.at[:, b], win.at[:, b], w_sems.at[n]) for n, b in enumerate(order)]
    load_o = [pltpu.make_async_copy(w_out.at[b], wout.at[b], o_sems.at[n]) for n, b in enumerate(order)]
    load_t = [pltpu.make_async_copy(tok.at[:, pl.ds(c * HALF, HALF)], gat.at[me, c, pl.ds(HEAD, ROWS)], own_sem.at[c])
              for c in range(2)]
    load_s = [pltpu.make_async_copy(src, dst, small_sems.at[n]) for n, (src, dst) in enumerate(
        ((rate_hbm, rate), (residue_hbm, residue), (taps_hbm, taps)))]

    barrier = pltpu.get_barrier_semaphore()

    def greet(sem, where):
        pl.semaphore_signal(sem, inc=1, device_id=where, device_id_type=MESH)

    def chip(step, of_core):
        return (ctx, lax.rem(x + step, 4) * 2 + of_core)

    @pl.when(core == 0)
    def _():
        greet(barrier, chip(1, 0))
        greet(barrier, chip(3, 0))

    @pl.when(core == 1)
    def _():
        for step in (0, 1, 3):
            greet(barrier, chip(step, 0))

    for c in load_t + load_s + load_w + load_o:
        c.start()

    @pl.when(core == 0)
    def _():
        pl.semaphore_wait(barrier, 5)
        greet(ready, chip(0, 1))
        greet(ring_in, chip(1, 1))
        greet(ring_in, chip(3, 1))

    @pl.when(core == 1)
    def _():
        pl.semaphore_wait(ready, 1)

    ring = (me, at(3), at(1), at(2), dev)
    g1 = Gather(lambda c, h: tok.at[pl.ds(h * TALL, TALL), pl.ds(c * HALF, HALF)],
                lambda b, c, h: gat.at[b, c, pl.ds(HEAD + h * TALL, TALL)], *ring, send1, recv1)
    g1.begin(0)
    g1.begin(1)

    even = lax.rem(x, 2) == 0

    @pl.when(core == 1)
    def _():
        pl.semaphore_wait(ring_in, 2)

    @pl.when((core == 1) & even & (ctx > 0))
    def _():
        greet(barrier, (ctx - 1, me))

    for c in load_t:
        c.wait()
    row16 = lax.broadcasted_iota(jnp.int32, (HEAD, LANES), 0)
    packed = jnp.zeros((HEAD, LANES), F32)
    for t in range(TILES):
        last = gat[me, t // 2, ROWS:ROWS + HEAD, t % 2 * LANES:(t % 2 + 1) * LANES].astype(F32)
        packed = jnp.where(row16 // 2 == t, pltpu.roll(last, 2 * t + 2, 0), packed)
    halo_out[...] = packed.astype(BF16)
    halos = [remote(halo_out, halo_in.at[me], halo_send.at[o], halo_recv.at[me],
                    (lax.rem(ctx + 1, CTX), lax.rem(me + o, BLOCKS))) for o in range(BLOCKS)]

    def send_halo(now):
        @pl.when(now & (core == 1) & even)
        def _():
            pl.semaphore_wait(barrier, 1)
            for where in (chip(0, 0), chip(1, 0), chip(1, 1)):
                greet(next_in, where)

        @pl.when(now & jnp.logical_not((core == 1) & even))
        def _():
            pl.semaphore_wait(next_in, 1)

        @pl.when(now)
        def _():
            for c in halos:
                c.start()

    waits_long = lax.rem(ctx, 4) != 3
    send_halo((ctx < CTX - 1) & jnp.logical_not(waits_long))

    for back in range(1, CTX):
        @pl.when((core == 1) & jnp.logical_not(even) & (ctx >= back))
        def _():
            greet(barrier, (ctx - back, me))

    for c in load_s:
        c.wait()

    decay[0] = jnp.exp(-rate[...])
    for n, power in enumerate((8, 32, 64, 128, 256)):
        decay[n + 1] = jnp.exp(-rate[...] * float(power))
    weight[...] = residue[...] * jnp.sqrt(1.0 - jnp.exp(-2.0 * rate[...]))
    sublane = lax.broadcasted_iota(jnp.int32, (8, WIDE), 0).astype(F32)
    for r in range(MODES):
        ramp[r] = jnp.exp(-rate[r:r + 1] * (sublane + 1.0)) * weight[r:r + 1]
        run_decay[r] = jnp.exp(-rate[r:r + 1] * (float(SUB) * (float(RUNS - 1) - sublane)))

    def halves_of(store, b, part, rows):
        if part is None:
            return jnp.concatenate([store[b, 0, rows], store[b, 1, rows]], 1)
        return store[b, part, rows]

    ALL, BODY, TOP = slice(0, HEAD + ROWS), slice(HEAD, HEAD + ROWS), slice(0, HEAD)

    def project(n, part=None, rows=ALL, fresh=False, slots=(0, 1, 2), last=False):
        b = order[n]
        cols = slice(0, WIDE) if part is None else slice(part * HALF, (part + 1) * HALF)
        for s in slots:
            value = jnp.dot(halves_of(gat, b, part, rows), win[s, b, cols], preferred_element_type=F32)
            if not fresh:
                value = acc[s, rows] + value
            if last:
                value = value.astype(BF16).astype(F32)
            acc[s, rows] = value

    def take_halo():
        acc[:, TOP] = jnp.zeros((3, HEAD, WIDE), F32)

        @pl.when(ctx > 0)
        def _():
            for q in range(BLOCKS):
                remote(halo_out, halo_in.at[q], halo_send.at[0], halo_recv.at[q], dev(1)).wait_recv()
                rows = halo_in[q].astype(F32)
                for t in range(TILES):
                    gat[q, t // 2, 0:HEAD, t % 2 * LANES:(t % 2 + 1) * LANES] = pltpu.roll(
                        rows, HEAD - 2 - 2 * t, 0).astype(BF16)

        @pl.when(ctx == 0)
        def _():
            for q in range(BLOCKS):
                gat[q, :, 0:HEAD] = jnp.zeros((2, HEAD, HALF), BF16)

    def project_own():
        send_halo((ctx < CTX - 1) & waits_long)
        load_w[0].wait()
        project(0, rows=BODY, fresh=True)

    def project_other():
        load_w[1].wait()
        for c in range(2):
            g1.wait_side([g1.own], c)
        project(1, rows=BODY)

    def project_near():
        load_w[2].wait()
        project(2, rows=BODY)
        load_w[3].wait()
        project(3, rows=BODY)

    def project_near_other():
        hear_later()
        take_halo()
        for c in range(2):
            g1.wait_side([g1.side_l, g1.side_r], c)
        load_w[4].wait()
        project(4)
        load_w[5].wait()
        project(5)

    def project_far():
        for n in range(4):
            project(n, rows=TOP)
        load_w[6].wait()
        project(6)
        load_w[7].wait()
        g1.wait_side([g1.side_f], 0)
        project(7, 0)
        g1.wait_side([g1.side_f], 1)
        project(7, 1, slots=(1, 2), last=True)

    def hear_later():
        @pl.when((ctx < CTX - 1) & (core == 1) & jnp.logical_not(even))
        def _():
            pl.semaphore_wait(barrier, CTX - 1 - ctx)
            for where in (chip(0, 0), chip(3, 0), chip(3, 1)):
                greet(later_in, where)

    def idle():
        pass

    g1.relay((idle, project_own, project_other, idle, project_near, project_near_other, project_far))

    def filtered(s, q, lanes):
        value = None
        for tap in range(SHORT):
            first = HEAD + SUB * q - tap
            term = taps[tap, s:s + 1, lanes] * acc[s, first:first + SUB, lanes]
            value = term if value is None else value + term
        return value

    row = lax.broadcasted_iota(jnp.int32, (8, LANES), 0)

    def spread(ref, r, lanes):
        return jnp.broadcast_to(ref[r:r + 1, lanes], (8, LANES))

    def columns(half):
        return slice(SPLIT[half] * LANES, SPLIT[half + 1] * LANES)

    def lanes_of(tile):
        return pl.ds(pl.multiple_of(tile * LANES, LANES), LANES)

    def block_state(half):
        for t in range(SPLIT[half], SPLIT[half + 1]):
            lanes = slice(t * LANES, (t + 1) * LANES)
            for q in range(RUNS):
                gated[t, SUB * q:SUB * (q + 1)] = (
                    filtered(1, q, lanes) * filtered(2, q, lanes)).astype(BF16).astype(F32)

        @pl.loop(SPLIT[half], SPLIT[half + 1])
        def _(tile):
            lanes = lanes_of(tile)
            d = [spread(decay.at[0], r, lanes) for r in range(MODES)]

            def step(j, states):
                g = gated[tile, pl.ds(j, RUNS, stride=SUB)]
                return tuple(d[r] * states[r] + g for r in range(MODES))

            states = lax.fori_loop(0, SUB, step, tuple(jnp.zeros((8, LANES), F32) for _ in range(MODES)), unroll=32)
            where = pl.ds(pl.multiple_of((tile - SPLIT[half]) * LANES, LANES), LANES)
            for r in range(MODES):
                run_state[r, :, lanes] = states[r]
                state_out[half][r:r + 1, where] = jnp.sum(
                    run_decay[r, :, lanes] * states[r], axis=0, keepdims=True).astype(STATE)

        if half == 0:
            @pl.when((ctx < CTX - 1) & jnp.logical_not((core == 1) & jnp.logical_not(even)))
            def _():
                pl.semaphore_wait(later_in, 1)

        for ahead in range(1, CTX):
            @pl.when(ctx + ahead < CTX)
            def _():
                remote(state_out[half], state_in[half].at[ctx], state_send.at[half, ahead], state_recv.at[half, ctx],
                       (lax.rem(ctx + ahead, CTX), me)).start()

    block_state(0)
    block_state(1)
    project(7, 1, slots=(0,), last=True)

    def own_part(half):
        for t in range(SPLIT[half], SPLIT[half + 1]):
            lanes = slice(t * LANES, (t + 1) * LANES)
            for q in range(RUNS):
                gate0[t, SUB * q:SUB * (q + 1)] = filtered(0, q, lanes)

        @pl.loop(SPLIT[half], SPLIT[half + 1])
        def _(tile):
            lanes = lanes_of(tile)
            before = []
            for r in range(MODES):
                s = run_state[r, :, lanes]
                for n, shift in enumerate((1, 2, 4)):
                    s = s + jnp.where(row >= shift, spread(decay.at[2 + n], r, lanes) * pltpu.roll(s, shift, 0), 0.0)
                before.append(jnp.where(row >= 1, pltpu.roll(s, 1, 0), 0.0))
            d = [spread(decay.at[0], r, lanes) for r in range(MODES)]
            w = [spread(weight, r, lanes) for r in range(MODES)]

            def step(j, states):
                g = gated[tile, pl.ds(j, RUNS, stride=SUB)]
                sums = [None] * 4
                after = []
                for r in range(MODES):
                    s = d[r] * states[r] + g
                    after.append(s)
                    term = w[r] * s
                    sums[r % 4] = term if sums[r % 4] is None else sums[r % 4] + term
                conv[tile, pl.ds(j, RUNS, stride=SUB)] = total_of(sums)
                return tuple(after)

            lax.fori_loop(0, SUB, step, tuple(before), unroll=8)

    def merge(half):
        def add(j, value):
            remote(state_out[half], state_in[half].at[j], state_send.at[half, 0], state_recv.at[half, j],
                   dev(1)).wait_recv()
            return decay[5, :, columns(half)] * value + state_in[half][j].astype(F32)

        cols = columns(half)
        entry[:, cols] = lax.fori_loop(0, ctx, add, jnp.zeros((MODES, cols.stop - cols.start), F32))

    def modulate(half, high):
        @pl.loop(SPLIT[half], SPLIT[half + 1])
        def _(tile):
            lanes = lanes_of(tile)
            if high == 0:
                z = tuple(ramp[r, :, lanes] * entry[r:r + 1, lanes] for r in range(MODES))
            else:
                z = tuple(run_state[r, :, lanes] for r in range(MODES))
            d8 = [spread(decay.at[1], r, lanes) for r in range(MODES)]

            def step(q, z):
                halves = []
                for part in range(2):
                    rows = pl.ds(pl.multiple_of(q * 16 + part * 8, 8), 8)
                    halves.append(gate0[tile, rows] * (conv[tile, rows] + total_of(list(z))))
                    z = tuple(d8[r] * z[r] for r in range(MODES))
                mod[me, pl.ds(pl.multiple_of(q * 16, 16), 16), lanes] = jnp.concatenate(halves, 0).astype(BF16)
                return z

            z = lax.fori_loop(high * TALL // 16, (high + 1) * TALL // 16, step, z, unroll=2)
            if high == 0:
                for r in range(MODES):
                    run_state[r, :, lanes] = z[r]

    def place(b, c, h):
        cols = columns(c)
        return mod.at[b, pl.ds(h * TALL, TALL), pl.ds(cols.start, cols.stop - cols.start)]

    g2 = Gather(lambda c, h: place(me, c, h), place, *ring, send2, recv2)
    for half in range(2):
        own_part(half)
        merge(half)
        modulate(half, 0)
        g2.begin_rows(half, 0)
        modulate(half, 1)
        g2.begin_rows(half, 1)

    def mix(n, part=None, fresh=False):
        b = order[n]
        cols = slice(0, WIDE) if part is None else columns(part)
        value = jnp.dot(mod[b, :, cols], wout[b, cols], preferred_element_type=F32)
        total[...] = value if fresh else total[...] + value

    def settle():
        g1.finish()

        @pl.when(ctx < CTX - 1)
        def _():
            for c in halos:
                c.wait_send()

        for half in range(2):
            for ahead in range(1, CTX):
                @pl.when(ctx + ahead < CTX)
                def _():
                    remote(state_out[half], state_in[half].at[ctx], state_send.at[half, ahead],
                           state_recv.at[half, ctx], (lax.rem(ctx + ahead, CTX), me)).wait_send()

    def mix_own():
        for c in load_o:
            c.wait()
        mix(0, fresh=True)

    def mix_other():
        for c in range(2):
            g2.wait_side([g2.own], c)
        mix(1)

    def mix_near():
        mix(2)
        mix(3)

    def mix_near_other():
        for c in range(2):
            g2.wait_side([g2.side_l, g2.side_r], c)
        mix(4)
        mix(5)
        mix(6, 0)

    def mix_far():
        g2.wait_side([g2.side_f], 0)
        mix(7, 0)
        mix(6, 1)
        g2.finish(late=False)
        g2.wait_side([g2.side_f], 1)
        b = order[7]
        out[...] = (total[...] + jnp.dot(
            mod[b, :, columns(1)], wout[b, columns(1)], preferred_element_type=F32)).astype(BF16)

    g2.relay((idle, mix_own, mix_other, settle, mix_near, mix_near_other, mix_far))

    g2.finish(late=True)


def per_device(tokens, w_in, short_kernel, residue, rate, w_out):
    w_in = jnp.transpose(w_in, (1, 0, 2)).reshape(3, BLOCKS, WIDE, WIDE)
    w_out = w_out.reshape(BLOCKS, WIDE, WIDE)
    dma = pltpu.SemaphoreType.DMA
    vmem = pltpu.VMEM
    return pl.pallas_call(
        kernel,
        out_shape=pltpu.VMEM((ROWS, WIDE), BF16),
        in_specs=[pl.BlockSpec(memory_space=pltpu.HBM)] * 6,
        out_specs=pl.BlockSpec(memory_space=pltpu.VMEM),
        scratch_shapes=[
            vmem((SHORT, 3, WIDE), F32),
            vmem((MODES, WIDE), F32),
            vmem((MODES, WIDE), F32),
            vmem((3, BLOCKS, WIDE, WIDE), BF16),
            vmem((BLOCKS, WIDE, WIDE), BF16),
            vmem((BLOCKS, 2, HEAD + ROWS, HALF), BF16),
            vmem((BLOCKS, ROWS, WIDE), BF16),
            vmem((3, HEAD + ROWS, WIDE), F32),
            vmem((ROWS, WIDE), F32),
            vmem((TILES, ROWS + SUB, LANES), F32),
            vmem((TILES, ROWS + SUB, LANES), F32),
            vmem((TILES, ROWS, LANES), F32),
            vmem((6, MODES, WIDE), F32),
            vmem((MODES, WIDE), F32),
            vmem((MODES, 8, WIDE), F32),
            vmem((MODES, 8, WIDE), F32),
            vmem((MODES, 8, WIDE), F32),
            vmem((HEAD, LANES), BF16),
            vmem((BLOCKS, HEAD, LANES), BF16),
            *[vmem((MODES, (SPLIT[h + 1] - SPLIT[h]) * LANES), STATE) for h in range(2)],
            *[vmem((CTX, MODES, (SPLIT[h + 1] - SPLIT[h]) * LANES), STATE) for h in range(2)],
            vmem((MODES, WIDE), F32),
            dma((BLOCKS,)), dma((BLOCKS,)), dma((2,)), dma((3,)),
            dma((32,)), dma((32,)), dma((32,)), dma((32,)),
            dma((BLOCKS,)), dma((BLOCKS,)),
            dma((2, CTX)), dma((2, CTX)),
            pltpu.SemaphoreType.REGULAR, pltpu.SemaphoreType.REGULAR, pltpu.SemaphoreType.REGULAR,
            pltpu.SemaphoreType.REGULAR,
        ],
        compiler_params=pltpu.CompilerParams(
            collective_id=0, has_side_effects=True, vmem_limit_bytes=60 * 2**20),
        cost_estimate=pl.CostEstimate(
            flops=2 * ROWS * 4096 * 2048, bytes_accessed=17 * 2**20, transcendentals=0),
    )(tokens, w_in, short_kernel, residue.T, rate.T, w_out)


def solution(mesh):
    in_specs = (
        P("ctx", "chan"),
        P(None, None, "chan"),
        P(None, None, "chan"),
        P("chan", None),
        P("chan", None),
        P(None, "chan"),
    )
    return jax.shard_map(
        per_device, mesh=mesh, in_specs=in_specs, out_specs=P("ctx", "chan"), check_vma=False)
```

```python
import jax
import jax.numpy as jnp
from jax import lax
from jax.experimental import pallas as pl
from jax.experimental.pallas import tpu as pltpu
from jax.sharding import PartitionSpec as P

MESH = pl.DeviceIdType.MESH
F32 = jnp.float32
BF16 = jnp.bfloat16
STATE = jnp.bfloat16
CTX = 16
ROWS = 256
WIDE = 512
BLOCKS = 8
MODES = 16
SHORT = 3
RUNS = 8
SUB = ROWS // RUNS
LANES = 128
TILES = WIDE // LANES
HALF = WIDE // 2
TALL = ROWS // 2
HEAD = 16
SPLIT = (0, 2, TILES)


def remote(src, dst, send, recv, where):
    return pltpu.make_async_remote_copy(
        src_ref=src, dst_ref=dst, send_sem=send, recv_sem=recv, device_id=where, device_id_type=MESH)


class Gather:
    def __init__(self, source, here, block, left, right, far, dev, send, recv):
        count = [0]

        def copy(src, dst, where):
            s = count[0]
            count[0] += 1
            return remote(src, dst, send.at[s], recv.at[s], where)

        quarters = [(c, h) for c in range(2) for h in range(2)]
        to_right, to_left, to_other = dev(1), dev(3), dev(0, True)
        self.right = {q: copy(source(*q), here(block, *q), to_right) for q in quarters}
        self.left = {q: copy(source(*q), here(block, *q), to_left) for q in quarters}
        self.own = {q: copy(source(*q), here(block, *q), to_other) for q in quarters}
        self.on_right = [copy(here(left, c, 0), here(left, c, 0), to_right) for c in range(2)]
        self.on_left = [copy(here(right, c, 1), here(right, c, 1), to_left) for c in range(2)]
        self.side_l = {q: copy(here(left, *q), here(left, *q), to_other) for q in quarters}
        self.side_r = {q: copy(here(right, *q), here(right, *q), to_other) for q in quarters}
        self.side_f = {q: copy(here(far, *q), here(far, *q), to_other) for q in quarters}

    def begin(self, c):
        for h in range(2):
            self.right[c, h].start()
            self.left[c, 1 - h].start()
        for h in range(2):
            self.own[c, h].start()

    def begin_rows(self, c, h):
        self.right[c, h].start()
        if h == 1:
            self.left[c, 1].start()
            self.left[c, 0].start()
        self.own[c, h].start()

    def relay(self, work):
        work[0]()
        for c in range(2):
            self.right[c, 0].wait_recv()
            self.on_right[c].start()
            self.side_l[c, 0].start()
            self.left[c, 1].wait_recv()
            self.on_left[c].start()
            self.side_r[c, 1].start()
            work[1 + 2 * c]()
            self.right[c, 1].wait_recv()
            self.side_l[c, 1].start()
            self.left[c, 0].wait_recv()
            self.side_r[c, 0].start()
            work[2 + 2 * c]()
        for c in range(2):
            self.on_right[c].wait_recv()
            self.side_f[c, 0].start()
            self.on_left[c].wait_recv()
            self.side_f[c, 1].start()
            work[5 + c]()

    def wait_side(self, sides, c):
        for side in sides:
            for h in range(2):
                side[c, h].wait_recv()

    def finish(self, late=None):
        early = [self.right, self.left, self.own, self.side_l, self.side_r]
        if late is not True:
            for group in early:
                for c in group.values():
                    c.wait_send()
        if late is not False:
            for c in list(self.side_f.values()) + self.on_right + self.on_left:
                c.wait_send()


def total_of(terms):
    while len(terms) > 1:
        terms = [a + b for a, b in zip(terms[::2], terms[1::2])]
    return terms[0]


def kernel(tok, w_in, taps_hbm, residue_hbm, rate_hbm, w_out, out,
           taps, residue, rate, win, wout, gat, mod, acc, total, gated, conv, gate0,
           decay, weight, run_state, run_decay, ramp, halo_out, halo_in, state_out0, state_out1, state_in0, state_in1, entry,
           w_sems, o_sems, own_sem, small_sems, send1, recv1, send2, recv2, halo_send, halo_recv,
           state_send, state_recv, ready, ring_in, next_in, later_in):
    state_out, state_in = (state_out0, state_out1), (state_in0, state_in1)
    me = lax.axis_index("chan")
    ctx = lax.axis_index("ctx")
    x, core = me // 2, me % 2

    def at(step, flip=False):
        return lax.rem(x + step, 4) * 2 + (1 - core if flip else core)

    def dev(step, flip=False):
        return (ctx, at(step, flip))

    order = [me, at(0, True), at(3), at(1), at(3, True), at(1, True), at(2), at(2, True)]

    load_w = [pltpu.make_async_copy(w_in.at[:, b], win.at[:, b], w_sems.at[n]) for n, b in enumerate(order)]
    load_o = [pltpu.make_async_copy(w_out.at[b], wout.at[b], o_sems.at[n]) for n, b in enumerate(order)]
    load_t = [pltpu.make_async_copy(tok.at[:, pl.ds(c * HALF, HALF)], gat.at[me, c, pl.ds(HEAD, ROWS)], own_sem.at[c])
              for c in range(2)]
    load_s = [pltpu.make_async_copy(src, dst, small_sems.at[n]) for n, (src, dst) in enumerate(
        ((rate_hbm, rate), (residue_hbm, residue), (taps_hbm, taps)))]

    barrier = pltpu.get_barrier_semaphore()

    def greet(sem, where):
        pl.semaphore_signal(sem, inc=1, device_id=where, device_id_type=MESH)

    def chip(step, of_core):
        return (ctx, lax.rem(x + step, 4) * 2 + of_core)

    @pl.when(core == 0)
    def _():
        greet(barrier, chip(1, 0))
        greet(barrier, chip(3, 0))

    @pl.when(core == 1)
    def _():
        for step in (0, 1, 3):
            greet(barrier, chip(step, 0))

    for c in load_t + load_s:
        c.start()

    @pl.when(core == 0)
    def _():
        pl.semaphore_wait(barrier, 5)
        greet(ready, chip(0, 1))
        greet(ring_in, chip(1, 1))
        greet(ring_in, chip(3, 1))

    @pl.when(core == 1)
    def _():
        pl.semaphore_wait(ready, 1)

    ring = (me, at(3), at(1), at(2), dev)
    def place_token(b, c, h):
        return gat.at[b, c, pl.ds(HEAD + h * TALL, TALL)]

    for c in load_t:
        c.wait()
    g1 = Gather(lambda c, h: place_token(me, c, h), place_token, *ring, send1, recv1)
    g1.begin(0)
    g1.begin(1)
    for c in load_w:
        c.start()

    even = lax.rem(x, 2) == 0

    @pl.when(core == 1)
    def _():
        pl.semaphore_wait(ring_in, 2)

    @pl.when((core == 1) & even & (ctx > 0))
    def _():
        greet(barrier, (ctx - 1, me))

    row16 = lax.broadcasted_iota(jnp.int32, (HEAD, LANES), 0)
    packed = jnp.zeros((HEAD, LANES), F32)
    for t in range(TILES):
        last = gat[me, t // 2, ROWS:ROWS + HEAD, t % 2 * LANES:(t % 2 + 1) * LANES].astype(F32)
        packed = jnp.where(row16 // 2 == t, pltpu.roll(last, 2 * t + 2, 0), packed)
    halo_out[...] = packed.astype(BF16)
    halos = [remote(halo_out, halo_in.at[me], halo_send.at[o], halo_recv.at[me],
                    (lax.rem(ctx + 1, CTX), lax.rem(me + o, BLOCKS))) for o in range(BLOCKS)]

    def send_halo(now):
        @pl.when(now & (core == 1) & even)
        def _():
            pl.semaphore_wait(barrier, 1)
            for where in (chip(0, 0), chip(1, 0), chip(1, 1)):
                greet(next_in, where)

        @pl.when(now & jnp.logical_not((core == 1) & even))
        def _():
            pl.semaphore_wait(next_in, 1)

        @pl.when(now)
        def _():
            for c in halos:
                c.start()

    waits_long = lax.rem(ctx, 4) != 3
    send_halo((ctx < CTX - 1) & jnp.logical_not(waits_long))

    for back in range(1, CTX):
        @pl.when((core == 1) & jnp.logical_not(even) & (ctx >= back))
        def _():
            greet(barrier, (ctx - back, me))

    for c in load_s:
        c.wait()

    decay[0] = jnp.exp(-rate[...])
    for n, power in enumerate((8, 32, 64, 128, 256)):
        decay[n + 1] = jnp.exp(-rate[...] * float(power))
    weight[...] = residue[...] * jnp.sqrt(1.0 - jnp.exp(-2.0 * rate[...]))
    sublane = lax.broadcasted_iota(jnp.int32, (8, WIDE), 0).astype(F32)
    for r in range(MODES):
        ramp[r] = jnp.exp(-rate[r:r + 1] * (sublane + 1.0)) * weight[r:r + 1]
        run_decay[r] = jnp.exp(-rate[r:r + 1] * (float(SUB) * (float(RUNS - 1) - sublane)))

    def halves_of(store, b, part, rows):
        if part is None:
            return jnp.concatenate([store[b, 0, rows], store[b, 1, rows]], 1)
        return store[b, part, rows]

    ALL, BODY, TOP = slice(0, HEAD + ROWS), slice(HEAD, HEAD + ROWS), slice(0, HEAD)

    def project(n, part=None, rows=ALL, fresh=False, slots=(0, 1, 2), last=False):
        b = order[n]
        cols = slice(0, WIDE) if part is None else slice(part * HALF, (part + 1) * HALF)
        for s in slots:
            value = jnp.dot(halves_of(gat, b, part, rows), win[s, b, cols], preferred_element_type=F32)
            if not fresh:
                value = acc[s, rows] + value
            if last:
                value = value.astype(BF16).astype(F32)
            acc[s, rows] = value

    def take_halo():
        acc[:, TOP] = jnp.zeros((3, HEAD, WIDE), F32)

        @pl.when(ctx > 0)
        def _():
            for q in range(BLOCKS):
                remote(halo_out, halo_in.at[q], halo_send.at[0], halo_recv.at[q], dev(1)).wait_recv()
                rows = halo_in[q].astype(F32)
                for t in range(TILES):
                    gat[q, t // 2, 0:HEAD, t % 2 * LANES:(t % 2 + 1) * LANES] = pltpu.roll(
                        rows, HEAD - 2 - 2 * t, 0).astype(BF16)

        @pl.when(ctx == 0)
        def _():
            for q in range(BLOCKS):
                gat[q, :, 0:HEAD] = jnp.zeros((2, HEAD, HALF), BF16)

    def project_own():
        send_halo((ctx < CTX - 1) & waits_long)
        load_w[0].wait()
        project(0, rows=BODY, fresh=True)

    def project_other():
        load_w[1].wait()
        for c in range(2):
            g1.wait_side([g1.own], c)
        project(1, rows=BODY)

    def project_near():
        load_w[2].wait()
        project(2, rows=BODY)
        load_w[3].wait()
        project(3, rows=BODY)

    def project_near_other():
        hear_later()
        take_halo()
        for c in range(2):
            g1.wait_side([g1.side_l, g1.side_r], c)
        load_w[4].wait()
        project(4)
        load_w[5].wait()
        project(5)

    def project_far():
        for n in range(4):
            project(n, rows=TOP)
        load_w[6].wait()
        project(6)
        load_w[7].wait()
        g1.wait_side([g1.side_f], 0)
        project(7, 0)
        g1.wait_side([g1.side_f], 1)
        project(7, 1, slots=(1, 2), last=True)

    def hear_later():
        @pl.when((ctx < CTX - 1) & (core == 1) & jnp.logical_not(even))
        def _():
            pl.semaphore_wait(barrier, CTX - 1 - ctx)
            for where in (chip(0, 0), chip(3, 0), chip(3, 1)):
                greet(later_in, where)

    def idle():
        pass

    g1.relay((idle, project_own, project_other, idle, project_near, project_near_other, project_far))

    def filtered(s, q, lanes):
        value = None
        for tap in range(SHORT):
            first = HEAD + SUB * q - tap
            term = taps[tap, s:s + 1, lanes] * acc[s, first:first + SUB, lanes]
            value = term if value is None else value + term
        return value

    row = lax.broadcasted_iota(jnp.int32, (8, LANES), 0)

    def spread(ref, r, lanes):
        return jnp.broadcast_to(ref[r:r + 1, lanes], (8, LANES))

    def columns(half):
        return slice(SPLIT[half] * LANES, SPLIT[half + 1] * LANES)

    def lanes_of(tile):
        return pl.ds(pl.multiple_of(tile * LANES, LANES), LANES)

    def block_state(half):
        for t in range(SPLIT[half], SPLIT[half + 1]):
            lanes = slice(t * LANES, (t + 1) * LANES)
            for q in range(RUNS):
                gated[t, SUB * q:SUB * (q + 1)] = (
                    filtered(1, q, lanes) * filtered(2, q, lanes)).astype(BF16).astype(F32)

        @pl.loop(SPLIT[half], SPLIT[half + 1])
        def _(tile):
            lanes = lanes_of(tile)
            d = [spread(decay.at[0], r, lanes) for r in range(MODES)]

            def step(j, states):
                g = gated[tile, pl.ds(j, RUNS, stride=SUB)]
                return tuple(d[r] * states[r] + g for r in range(MODES))

            states = lax.fori_loop(0, SUB, step, tuple(jnp.zeros((8, LANES), F32) for _ in range(MODES)), unroll=32)
            where = pl.ds(pl.multiple_of((tile - SPLIT[half]) * LANES, LANES), LANES)
            for r in range(MODES):
                run_state[r, :, lanes] = states[r]
                state_out[half][r:r + 1, where] = jnp.sum(
                    run_decay[r, :, lanes] * states[r], axis=0, keepdims=True).astype(STATE)

        if half == 0:
            @pl.when((ctx < CTX - 1) & jnp.logical_not((core == 1) & jnp.logical_not(even)))
            def _():
                pl.semaphore_wait(later_in, 1)

        for ahead in range(1, CTX):
            @pl.when(ctx + ahead < CTX)
            def _():
                remote(state_out[half], state_in[half].at[ctx], state_send.at[half, ahead], state_recv.at[half, ctx],
                       (lax.rem(ctx + ahead, CTX), me)).start()

    for c in load_o:
        c.start()
    block_state(0)
    block_state(1)
    project(7, 1, slots=(0,), last=True)

    def own_part(half):
        for t in range(SPLIT[half], SPLIT[half + 1]):
            lanes = slice(t * LANES, (t + 1) * LANES)
            for q in range(RUNS):
                gate0[t, SUB * q:SUB * (q + 1)] = filtered(0, q, lanes)

        @pl.loop(SPLIT[half], SPLIT[half + 1])
        def _(tile):
            lanes = lanes_of(tile)
            before = []
            for r in range(MODES):
                s = run_state[r, :, lanes]
                for n, shift in enumerate((1, 2, 4)):
                    s = s + jnp.where(row >= shift, spread(decay.at[2 + n], r, lanes) * pltpu.roll(s, shift, 0), 0.0)
                before.append(jnp.where(row >= 1, pltpu.roll(s, 1, 0), 0.0))
            d = [spread(decay.at[0], r, lanes) for r in range(MODES)]
            w = [spread(weight, r, lanes) for r in range(MODES)]

            def step(j, states):
                g = gated[tile, pl.ds(j, RUNS, stride=SUB)]
                sums = [None] * 4
                after = []
                for r in range(MODES):
                    s = d[r] * states[r] + g
                    after.append(s)
                    term = w[r] * s
                    sums[r % 4] = term if sums[r % 4] is None else sums[r % 4] + term
                conv[tile, pl.ds(j, RUNS, stride=SUB)] = total_of(sums)
                return tuple(after)

            lax.fori_loop(0, SUB, step, tuple(before), unroll=8)

    def merge(half):
        def add(j, value):
            remote(state_out[half], state_in[half].at[j], state_send.at[half, 0], state_recv.at[half, j],
                   dev(1)).wait_recv()
            return decay[5, :, columns(half)] * value + state_in[half][j].astype(F32)

        cols = columns(half)
        entry[:, cols] = lax.fori_loop(0, ctx, add, jnp.zeros((MODES, cols.stop - cols.start), F32))

    def modulate(half, high):
        @pl.loop(SPLIT[half], SPLIT[half + 1])
        def _(tile):
            lanes = lanes_of(tile)
            if high == 0:
                z = tuple(ramp[r, :, lanes] * entry[r:r + 1, lanes] for r in range(MODES))
            else:
                z = tuple(run_state[r, :, lanes] for r in range(MODES))
            d8 = [spread(decay.at[1], r, lanes) for r in range(MODES)]

            def step(q, z):
                halves = []
                for part in range(2):
                    rows = pl.ds(pl.multiple_of(q * 16 + part * 8, 8), 8)
                    halves.append(gate0[tile, rows] * (conv[tile, rows] + total_of(list(z))))
                    z = tuple(d8[r] * z[r] for r in range(MODES))
                mod[me, pl.ds(pl.multiple_of(q * 16, 16), 16), lanes] = jnp.concatenate(halves, 0).astype(BF16)
                return z

            z = lax.fori_loop(high * TALL // 16, (high + 1) * TALL // 16, step, z, unroll=2)
            if high == 0:
                for r in range(MODES):
                    run_state[r, :, lanes] = z[r]

    def place(b, c, h):
        cols = columns(c)
        return mod.at[b, pl.ds(h * TALL, TALL), pl.ds(cols.start, cols.stop - cols.start)]

    g2 = Gather(lambda c, h: place(me, c, h), place, *ring, send2, recv2)
    for half in range(2):
        own_part(half)
        merge(half)
        modulate(half, 0)
        g2.begin_rows(half, 0)
        modulate(half, 1)
        g2.begin_rows(half, 1)

    def mix(n, part=None, fresh=False):
        b = order[n]
        cols = slice(0, WIDE) if part is None else columns(part)
        value = jnp.dot(mod[b, :, cols], wout[b, cols], preferred_element_type=F32)
        total[...] = value if fresh else total[...] + value

    def settle():
        g1.finish()

        @pl.when(ctx < CTX - 1)
        def _():
            for c in halos:
                c.wait_send()

        for half in range(2):
            for ahead in range(1, CTX):
                @pl.when(ctx + ahead < CTX)
                def _():
                    remote(state_out[half], state_in[half].at[ctx], state_send.at[half, ahead],
                           state_recv.at[half, ctx], (lax.rem(ctx + ahead, CTX), me)).wait_send()

    def mix_own():
        for c in load_o:
            c.wait()
        mix(0, fresh=True)

    def mix_other():
        for c in range(2):
            g2.wait_side([g2.own], c)
        mix(1)

    def mix_near():
        mix(2)
        mix(3)

    def mix_near_other():
        for c in range(2):
            g2.wait_side([g2.side_l, g2.side_r], c)
        mix(4)
        mix(5)
        mix(6, 0)

    def mix_far():
        g2.wait_side([g2.side_f], 0)
        mix(7, 0)
        mix(6, 1)
        g2.finish(late=False)
        g2.wait_side([g2.side_f], 1)
        b = order[7]
        out[...] = (total[...] + jnp.dot(
            mod[b, :, columns(1)], wout[b, columns(1)], preferred_element_type=F32)).astype(BF16)

    g2.relay((idle, mix_own, mix_other, settle, mix_near, mix_near_other, mix_far))

    g2.finish(late=True)


def per_device(tokens, w_in, short_kernel, residue, rate, w_out):
    w_in = jnp.transpose(w_in, (1, 0, 2)).reshape(3, BLOCKS, WIDE, WIDE)
    w_out = w_out.reshape(BLOCKS, WIDE, WIDE)
    dma = pltpu.SemaphoreType.DMA
    vmem = pltpu.VMEM
    return pl.pallas_call(
        kernel,
        out_shape=pltpu.VMEM((ROWS, WIDE), BF16),
        in_specs=[pl.BlockSpec(memory_space=pltpu.HBM)] * 6,
        out_specs=pl.BlockSpec(memory_space=pltpu.VMEM),
        scratch_shapes=[
            vmem((SHORT, 3, WIDE), F32),
            vmem((MODES, WIDE), F32),
            vmem((MODES, WIDE), F32),
            vmem((3, BLOCKS, WIDE, WIDE), BF16),
            vmem((BLOCKS, WIDE, WIDE), BF16),
            vmem((BLOCKS, 2, HEAD + ROWS, HALF), BF16),
            vmem((BLOCKS, ROWS, WIDE), BF16),
            vmem((3, HEAD + ROWS, WIDE), F32),
            vmem((ROWS, WIDE), F32),
            vmem((TILES, ROWS + SUB, LANES), F32),
            vmem((TILES, ROWS + SUB, LANES), F32),
            vmem((TILES, ROWS, LANES), F32),
            vmem((6, MODES, WIDE), F32),
            vmem((MODES, WIDE), F32),
            vmem((MODES, 8, WIDE), F32),
            vmem((MODES, 8, WIDE), F32),
            vmem((MODES, 8, WIDE), F32),
            vmem((HEAD, LANES), BF16),
            vmem((BLOCKS, HEAD, LANES), BF16),
            *[vmem((MODES, (SPLIT[h + 1] - SPLIT[h]) * LANES), STATE) for h in range(2)],
            *[vmem((CTX, MODES, (SPLIT[h + 1] - SPLIT[h]) * LANES), STATE) for h in range(2)],
            vmem((MODES, WIDE), F32),
            dma((BLOCKS,)), dma((BLOCKS,)), dma((2,)), dma((3,)),
            dma((32,)), dma((32,)), dma((32,)), dma((32,)),
            dma((BLOCKS,)), dma((BLOCKS,)),
            dma((2, CTX)), dma((2, CTX)),
            pltpu.SemaphoreType.REGULAR, pltpu.SemaphoreType.REGULAR, pltpu.SemaphoreType.REGULAR,
            pltpu.SemaphoreType.REGULAR,
        ],
        compiler_params=pltpu.CompilerParams(
            collective_id=0, has_side_effects=True, vmem_limit_bytes=60 * 2**20),
        cost_estimate=pl.CostEstimate(
            flops=2 * ROWS * 4096 * 2048, bytes_accessed=17 * 2**20, transcendentals=0),
    )(tokens, w_in, short_kernel, residue.T, rate.T, w_out)


def solution(mesh):
    in_specs = (
        P("ctx", "chan"),
        P(None, None, "chan"),
        P(None, None, "chan"),
        P("chan", None),
        P("chan", None),
        P(None, "chan"),
    )
    return jax.shard_map(
        per_device, mesh=mesh, in_specs=in_specs, out_specs=P("ctx", "chan"), check_vma=False)
```

```python
import jax
import jax.numpy as jnp
from jax import lax
from jax.experimental import pallas as pl
from jax.experimental.pallas import tpu as pltpu
from jax.sharding import PartitionSpec as P

MESH = pl.DeviceIdType.MESH
F32 = jnp.float32
BF16 = jnp.bfloat16
STATE = jnp.bfloat16
CTX = 16
ROWS = 256
WIDE = 512
BLOCKS = 8
MODES = 16
SHORT = 3
RUNS = 8
SUB = ROWS // RUNS
LANES = 128
TILES = WIDE // LANES
HALF = WIDE // 2
TALL = ROWS // 2
HEAD = 16
SPLIT = (0, 2, TILES)


def remote(src, dst, send, recv, where):
    return pltpu.make_async_remote_copy(
        src_ref=src, dst_ref=dst, send_sem=send, recv_sem=recv, device_id=where, device_id_type=MESH)


class Gather:
    def __init__(self, source, here, block, left, right, far, dev, send, recv):
        count = [0]

        def copy(src, dst, where):
            s = count[0]
            count[0] += 1
            return remote(src, dst, send.at[s], recv.at[s], where)

        quarters = [(c, h) for c in range(2) for h in range(2)]
        to_right, to_left, to_other = dev(1), dev(3), dev(0, True)
        self.right = {q: copy(source(*q), here(block, *q), to_right) for q in quarters}
        self.left = {q: copy(source(*q), here(block, *q), to_left) for q in quarters}
        self.own = {q: copy(source(*q), here(block, *q), to_other) for q in quarters}
        self.on_right = [copy(here(left, c, 0), here(left, c, 0), to_right) for c in range(2)]
        self.on_left = [copy(here(right, c, 1), here(right, c, 1), to_left) for c in range(2)]
        self.side_l = {q: copy(here(left, *q), here(left, *q), to_other) for q in quarters}
        self.side_r = {q: copy(here(right, *q), here(right, *q), to_other) for q in quarters}
        self.side_f = {q: copy(here(far, *q), here(far, *q), to_other) for q in quarters}

    def begin(self, c):
        for h in range(2):
            self.right[c, h].start()
            self.left[c, 1 - h].start()
        for h in range(2):
            self.own[c, h].start()

    def begin_rows(self, c, h):
        self.right[c, h].start()
        if h == 1:
            self.left[c, 1].start()
            self.left[c, 0].start()
        self.own[c, h].start()

    def relay(self, work):
        work[0]()
        for c in range(2):
            self.right[c, 0].wait_recv()
            self.on_right[c].start()
            self.side_l[c, 0].start()
            self.left[c, 1].wait_recv()
            self.on_left[c].start()
            self.side_r[c, 1].start()
            work[1 + 2 * c]()
            self.right[c, 1].wait_recv()
            self.side_l[c, 1].start()
            self.left[c, 0].wait_recv()
            self.side_r[c, 0].start()
            work[2 + 2 * c]()
        for c in range(2):
            self.on_right[c].wait_recv()
            self.side_f[c, 0].start()
            self.on_left[c].wait_recv()
            self.side_f[c, 1].start()
            work[5 + c]()

    def wait_side(self, sides, c):
        for side in sides:
            for h in range(2):
                side[c, h].wait_recv()

    def finish(self, late=None):
        early = [self.right, self.left, self.own, self.side_l, self.side_r]
        if late is not True:
            for group in early:
                for c in group.values():
                    c.wait_send()
        if late is not False:
            for c in list(self.side_f.values()) + self.on_right + self.on_left:
                c.wait_send()


def total_of(terms):
    while len(terms) > 1:
        terms = [a + b for a, b in zip(terms[::2], terms[1::2])]
    return terms[0]


def kernel(tok, w_in, taps_hbm, residue_hbm, rate_hbm, w_out, out,
           taps, residue, rate, win, wout, gat, mod, acc, total, gated, conv, gate0,
           decay, weight, run_state, run_decay, ramp, halo_out, halo_in, state_out0, state_out1, state_in0, state_in1, entry,
           w_sems, o_sems, own_sem, small_sems, send1, recv1, send2, recv2, halo_send, halo_recv,
           state_send, state_recv, ready, ring_in, next_in, later_in):
    state_out, state_in = (state_out0, state_out1), (state_in0, state_in1)
    me = lax.axis_index("chan")
    ctx = lax.axis_index("ctx")
    x, core = me // 2, me % 2

    def at(step, flip=False):
        return lax.rem(x + step, 4) * 2 + (1 - core if flip else core)

    def dev(step, flip=False):
        return (ctx, at(step, flip))

    order = [me, at(0, True), at(3), at(1), at(3, True), at(1, True), at(2), at(2, True)]

    load_w = [pltpu.make_async_copy(w_in.at[:, b], win.at[:, b], w_sems.at[n]) for n, b in enumerate(order)]
    load_o = [pltpu.make_async_copy(w_out.at[b], wout.at[b], o_sems.at[n]) for n, b in enumerate(order)]
    load_t = [pltpu.make_async_copy(tok.at[:, pl.ds(c * HALF, HALF)], gat.at[me, c, pl.ds(HEAD, ROWS)], own_sem.at[c])
              for c in range(2)]
    load_s = [pltpu.make_async_copy(src, dst, small_sems.at[n]) for n, (src, dst) in enumerate(
        ((rate_hbm, rate), (residue_hbm, residue), (taps_hbm, taps)))]

    barrier = pltpu.get_barrier_semaphore()

    def greet(sem, where):
        pl.semaphore_signal(sem, inc=1, device_id=where, device_id_type=MESH)

    def chip(step, of_core):
        return (ctx, lax.rem(x + step, 4) * 2 + of_core)

    @pl.when(core == 0)
    def _():
        greet(barrier, chip(1, 0))
        greet(barrier, chip(3, 0))

    @pl.when(core == 1)
    def _():
        for step in (0, 1, 3):
            greet(barrier, chip(step, 0))

    for c in load_t + load_s:
        c.start()

    @pl.when(core == 0)
    def _():
        pl.semaphore_wait(barrier, 5)
        greet(ready, chip(0, 1))
        greet(ring_in, chip(1, 1))
        greet(ring_in, chip(3, 1))

    @pl.when(core == 1)
    def _():
        pl.semaphore_wait(ready, 1)

    ring = (me, at(3), at(1), at(2), dev)
    def place_token(b, c, h):
        return gat.at[b, c, pl.ds(HEAD + h * TALL, TALL)]

    for c in load_t:
        c.wait()
    g1 = Gather(lambda c, h: place_token(me, c, h), place_token, *ring, send1, recv1)
    g1.begin(0)
    g1.begin(1)
    for c in load_w:
        c.start()

    even = lax.rem(x, 2) == 0

    @pl.when(core == 1)
    def _():
        pl.semaphore_wait(ring_in, 2)

    @pl.when((core == 1) & even & (ctx > 0))
    def _():
        greet(barrier, (ctx - 1, me))

    row16 = lax.broadcasted_iota(jnp.int32, (HEAD, LANES), 0)
    packed = jnp.zeros((HEAD, LANES), F32)
    for t in range(TILES):
        last = gat[me, t // 2, ROWS:ROWS + HEAD, t % 2 * LANES:(t % 2 + 1) * LANES].astype(F32)
        packed = jnp.where(row16 // 2 == t, pltpu.roll(last, 2 * t + 2, 0), packed)
    halo_out[...] = packed.astype(BF16)
    halos = [remote(halo_out, halo_in.at[me], halo_send.at[o], halo_recv.at[me],
                    (lax.rem(ctx + 1, CTX), lax.rem(me + o, BLOCKS))) for o in range(BLOCKS)]

    def send_halo(now):
        @pl.when(now & (core == 1) & even)
        def _():
            pl.semaphore_wait(barrier, 1)
            for where in (chip(0, 0), chip(1, 0), chip(1, 1)):
                greet(next_in, where)

        @pl.when(now & jnp.logical_not((core == 1) & even))
        def _():
            pl.semaphore_wait(next_in, 1)

        @pl.when(now)
        def _():
            for c in halos:
                c.start()

    waits_long = lax.rem(ctx, 4) != 3
    send_halo((ctx < CTX - 1) & jnp.logical_not(waits_long))

    for back in range(1, CTX):
        @pl.when((core == 1) & jnp.logical_not(even) & (ctx >= back))
        def _():
            greet(barrier, (ctx - back, me))

    for c in load_s:
        c.wait()

    decay[0] = jnp.exp(-rate[...])
    for n, power in enumerate((8, 32, 64, 128, 256)):
        decay[n + 1] = jnp.exp(-rate[...] * float(power))
    weight[...] = residue[...] * jnp.sqrt(1.0 - jnp.exp(-2.0 * rate[...]))
    sublane = lax.broadcasted_iota(jnp.int32, (8, WIDE), 0).astype(F32)
    for r in range(MODES):
        ramp[r] = jnp.exp(-rate[r:r + 1] * (sublane + 1.0)) * weight[r:r + 1]
        run_decay[r] = jnp.exp(-rate[r:r + 1] * (float(SUB) * (float(RUNS - 1) - sublane)))

    def halves_of(store, b, part, rows):
        if part is None:
            return jnp.concatenate([store[b, 0, rows], store[b, 1, rows]], 1)
        return store[b, part, rows]

    ALL, BODY, TOP = slice(0, HEAD + ROWS), slice(HEAD, HEAD + ROWS), slice(0, HEAD)

    def project(n, part=None, rows=ALL, fresh=False, slots=(0, 1, 2), last=False):
        b = order[n]
        cols = slice(0, WIDE) if part is None else slice(part * HALF, (part + 1) * HALF)
        for s in slots:
            value = jnp.dot(halves_of(gat, b, part, rows), win[s, b, cols], preferred_element_type=F32)
            if not fresh:
                value = acc[s, rows] + value
            if last:
                value = value.astype(BF16).astype(F32)
            acc[s, rows] = value

    def take_halo():
        acc[:, TOP] = jnp.zeros((3, HEAD, WIDE), F32)

        @pl.when(ctx > 0)
        def _():
            for q in range(BLOCKS):
                remote(halo_out, halo_in.at[q], halo_send.at[0], halo_recv.at[q], dev(1)).wait_recv()
                rows = halo_in[q].astype(F32)
                for t in range(TILES):
                    gat[q, t // 2, 0:HEAD, t % 2 * LANES:(t % 2 + 1) * LANES] = pltpu.roll(
                        rows, HEAD - 2 - 2 * t, 0).astype(BF16)

        @pl.when(ctx == 0)
        def _():
            for q in range(BLOCKS):
                gat[q, :, 0:HEAD] = jnp.zeros((2, HEAD, HALF), BF16)

    def project_own():
        send_halo((ctx < CTX - 1) & waits_long)
        load_w[0].wait()
        project(0, rows=BODY, fresh=True)

    def project_other():
        load_w[1].wait()
        for c in range(2):
            g1.wait_side([g1.own], c)
        project(1, rows=BODY)

    def project_near():
        load_w[2].wait()
        project(2, rows=BODY)
        load_w[3].wait()
        project(3, rows=BODY)

    def project_near_other():
        hear_later()
        take_halo()
        for c in range(2):
            g1.wait_side([g1.side_l, g1.side_r], c)
        load_w[4].wait()
        project(4)
        load_w[5].wait()
        project(5)

    def project_far():
        for n in range(4):
            project(n, rows=TOP)
        load_w[6].wait()
        project(6)
        load_w[7].wait()
        g1.wait_side([g1.side_f], 0)
        project(7, 0)
        g1.wait_side([g1.side_f], 1)
        project(7, 1, slots=(1, 2), last=True)

    def hear_later():
        @pl.when((ctx < CTX - 1) & (core == 1) & jnp.logical_not(even))
        def _():
            pl.semaphore_wait(barrier, CTX - 1 - ctx)
            for where in (chip(0, 0), chip(3, 0), chip(3, 1)):
                greet(later_in, where)

    def idle():
        pass

    g1.relay((idle, project_own, project_other, idle, project_near, project_near_other, project_far))

    def filtered(s, q, lanes):
        value = None
        for tap in range(SHORT):
            first = HEAD + SUB * q - tap
            term = taps[tap, s:s + 1, lanes] * acc[s, first:first + SUB, lanes]
            value = term if value is None else value + term
        return value

    row = lax.broadcasted_iota(jnp.int32, (8, LANES), 0)

    def spread(ref, r, lanes):
        return jnp.broadcast_to(ref[r:r + 1, lanes], (8, LANES))

    def columns(half):
        return slice(SPLIT[half] * LANES, SPLIT[half + 1] * LANES)

    def lanes_of(tile):
        return pl.ds(pl.multiple_of(tile * LANES, LANES), LANES)

    def block_state(half):
        for t in range(SPLIT[half], SPLIT[half + 1]):
            lanes = slice(t * LANES, (t + 1) * LANES)
            for q in range(RUNS):
                gated[t, SUB * q:SUB * (q + 1)] = (
                    filtered(1, q, lanes) * filtered(2, q, lanes)).astype(BF16).astype(F32)

        @pl.loop(SPLIT[half], SPLIT[half + 1])
        def _(tile):
            lanes = lanes_of(tile)
            d = [spread(decay.at[0], r, lanes) for r in range(MODES)]

            def step(j, states):
                g = gated[tile, pl.ds(j, RUNS, stride=SUB)]
                return tuple(d[r] * states[r] + g for r in range(MODES))

            states = lax.fori_loop(0, SUB, step, tuple(jnp.zeros((8, LANES), F32) for _ in range(MODES)), unroll=32)
            where = pl.ds(pl.multiple_of((tile - SPLIT[half]) * LANES, LANES), LANES)
            for r in range(MODES):
                run_state[r, :, lanes] = states[r]
                state_out[half][r:r + 1, where] = jnp.sum(
                    run_decay[r, :, lanes] * states[r], axis=0, keepdims=True).astype(STATE)

        if half == 0:
            @pl.when((ctx < CTX - 1) & jnp.logical_not((core == 1) & jnp.logical_not(even)))
            def _():
                pl.semaphore_wait(later_in, 1)

        for ahead in range(1, CTX):
            @pl.when(ctx + ahead < CTX)
            def _():
                remote(state_out[half], state_in[half].at[ctx], state_send.at[half, ahead], state_recv.at[half, ctx],
                       (lax.rem(ctx + ahead, CTX), me)).start()

    for c in load_o:
        c.start()
    block_state(0)
    block_state(1)
    project(7, 1, slots=(0,), last=True)

    def own_part(half):
        for t in range(SPLIT[half], SPLIT[half + 1]):
            lanes = slice(t * LANES, (t + 1) * LANES)
            for q in range(RUNS):
                gate0[t, SUB * q:SUB * (q + 1)] = filtered(0, q, lanes)

        @pl.loop(SPLIT[half], SPLIT[half + 1])
        def _(tile):
            lanes = lanes_of(tile)
            before = []
            for r in range(MODES):
                s = run_state[r, :, lanes]
                for n, shift in enumerate((1, 2, 4)):
                    s = s + jnp.where(row >= shift, spread(decay.at[2 + n], r, lanes) * pltpu.roll(s, shift, 0), 0.0)
                before.append(jnp.where(row >= 1, pltpu.roll(s, 1, 0), 0.0))
            d = [spread(decay.at[0], r, lanes) for r in range(MODES)]
            w = [spread(weight, r, lanes) for r in range(MODES)]

            def step(j, states):
                g = gated[tile, pl.ds(j, RUNS, stride=SUB)]
                sums = [None] * 4
                after = []
                for r in range(MODES):
                    s = d[r] * states[r] + g
                    after.append(s)
                    term = w[r] * s
                    sums[r % 4] = term if sums[r % 4] is None else sums[r % 4] + term
                conv[tile, pl.ds(j, RUNS, stride=SUB)] = total_of(sums)
                return tuple(after)

            lax.fori_loop(0, SUB, step, tuple(before), unroll=8)

    def merge(half):
        def add(j, value):
            remote(state_out[half], state_in[half].at[j], state_send.at[half, 0], state_recv.at[half, j],
                   dev(1)).wait_recv()
            return decay[5, :, columns(half)] * value + state_in[half][j].astype(F32)

        cols = columns(half)
        entry[:, cols] = lax.fori_loop(0, ctx, add, jnp.zeros((MODES, cols.stop - cols.start), F32))

    def modulate(half, high):
        @pl.loop(SPLIT[half], SPLIT[half + 1])
        def _(tile):
            lanes = lanes_of(tile)
            if high == 0:
                z = tuple(ramp[r, :, lanes] * entry[r:r + 1, lanes] for r in range(MODES))
            else:
                z = tuple(run_state[r, :, lanes] for r in range(MODES))
            d8 = [spread(decay.at[1], r, lanes) for r in range(MODES)]

            def step(q, z):
                halves = []
                for part in range(2):
                    rows = pl.ds(pl.multiple_of(q * 16 + part * 8, 8), 8)
                    halves.append(gate0[tile, rows] * (conv[tile, rows] + total_of(list(z))))
                    z = tuple(d8[r] * z[r] for r in range(MODES))
                mod[me, pl.ds(pl.multiple_of(q * 16, 16), 16), lanes] = jnp.concatenate(halves, 0).astype(BF16)
                return z

            z = lax.fori_loop(high * TALL // 16, (high + 1) * TALL // 16, step, z, unroll=2)
            if high == 0:
                for r in range(MODES):
                    run_state[r, :, lanes] = z[r]

    def place(b, c, h):
        cols = columns(c)
        return mod.at[b, pl.ds(h * TALL, TALL), pl.ds(cols.start, cols.stop - cols.start)]

    g2 = Gather(lambda c, h: place(me, c, h), place, *ring, send2, recv2)
    own_part(0)
    own_part(1)
    for half in range(2):
        merge(half)
        modulate(half, 0)
        g2.begin_rows(half, 0)
        modulate(half, 1)
        g2.begin_rows(half, 1)

    def mix(n, part=None, fresh=False):
        b = order[n]
        cols = slice(0, WIDE) if part is None else columns(part)
        value = jnp.dot(mod[b, :, cols], wout[b, cols], preferred_element_type=F32)
        total[...] = value if fresh else total[...] + value

    def settle():
        g1.finish()

        @pl.when(ctx < CTX - 1)
        def _():
            for c in halos:
                c.wait_send()

        for half in range(2):
            for ahead in range(1, CTX):
                @pl.when(ctx + ahead < CTX)
                def _():
                    remote(state_out[half], state_in[half].at[ctx], state_send.at[half, ahead],
                           state_recv.at[half, ctx], (lax.rem(ctx + ahead, CTX), me)).wait_send()

    def mix_own():
        for c in load_o:
            c.wait()
        mix(0, fresh=True)

    def mix_other():
        for c in range(2):
            g2.wait_side([g2.own], c)
        mix(1)

    def mix_near():
        mix(2)
        mix(3)

    def mix_near_other():
        for c in range(2):
            g2.wait_side([g2.side_l, g2.side_r], c)
        mix(4)
        mix(5)
        mix(6, 0)

    def mix_far():
        g2.wait_side([g2.side_f], 0)
        mix(7, 0)
        mix(6, 1)
        g2.finish(late=False)
        g2.wait_side([g2.side_f], 1)
        b = order[7]
        out[...] = (total[...] + jnp.dot(
            mod[b, :, columns(1)], wout[b, columns(1)], preferred_element_type=F32)).astype(BF16)

    g2.relay((idle, mix_own, mix_other, settle, mix_near, mix_near_other, mix_far))

    g2.finish(late=True)


def per_device(tokens, w_in, short_kernel, residue, rate, w_out):
    w_in = jnp.transpose(w_in, (1, 0, 2)).reshape(3, BLOCKS, WIDE, WIDE)
    w_out = w_out.reshape(BLOCKS, WIDE, WIDE)
    dma = pltpu.SemaphoreType.DMA
    vmem = pltpu.VMEM
    return pl.pallas_call(
        kernel,
        out_shape=pltpu.VMEM((ROWS, WIDE), BF16),
        in_specs=[pl.BlockSpec(memory_space=pltpu.HBM)] * 6,
        out_specs=pl.BlockSpec(memory_space=pltpu.VMEM),
        scratch_shapes=[
            vmem((SHORT, 3, WIDE), F32),
            vmem((MODES, WIDE), F32),
            vmem((MODES, WIDE), F32),
            vmem((3, BLOCKS, WIDE, WIDE), BF16),
            vmem((BLOCKS, WIDE, WIDE), BF16),
            vmem((BLOCKS, 2, HEAD + ROWS, HALF), BF16),
            vmem((BLOCKS, ROWS, WIDE), BF16),
            vmem((3, HEAD + ROWS, WIDE), F32),
            vmem((ROWS, WIDE), F32),
            vmem((TILES, ROWS + SUB, LANES), F32),
            vmem((TILES, ROWS + SUB, LANES), F32),
            vmem((TILES, ROWS, LANES), F32),
            vmem((6, MODES, WIDE), F32),
            vmem((MODES, WIDE), F32),
            vmem((MODES, 8, WIDE), F32),
            vmem((MODES, 8, WIDE), F32),
            vmem((MODES, 8, WIDE), F32),
            vmem((HEAD, LANES), BF16),
            vmem((BLOCKS, HEAD, LANES), BF16),
            *[vmem((MODES, (SPLIT[h + 1] - SPLIT[h]) * LANES), STATE) for h in range(2)],
            *[vmem((CTX, MODES, (SPLIT[h + 1] - SPLIT[h]) * LANES), STATE) for h in range(2)],
            vmem((MODES, WIDE), F32),
            dma((BLOCKS,)), dma((BLOCKS,)), dma((2,)), dma((3,)),
            dma((32,)), dma((32,)), dma((32,)), dma((32,)),
            dma((BLOCKS,)), dma((BLOCKS,)),
            dma((2, CTX)), dma((2, CTX)),
            pltpu.SemaphoreType.REGULAR, pltpu.SemaphoreType.REGULAR, pltpu.SemaphoreType.REGULAR,
            pltpu.SemaphoreType.REGULAR,
        ],
        compiler_params=pltpu.CompilerParams(
            collective_id=0, has_side_effects=True, vmem_limit_bytes=60 * 2**20),
        cost_estimate=pl.CostEstimate(
            flops=2 * ROWS * 4096 * 2048, bytes_accessed=17 * 2**20, transcendentals=0),
    )(tokens, w_in, short_kernel, residue.T, rate.T, w_out)


def solution(mesh):
    in_specs = (
        P("ctx", "chan"),
        P(None, None, "chan"),
        P(None, None, "chan"),
        P("chan", None),
        P("chan", None),
        P(None, "chan"),
    )
    return jax.shard_map(
        per_device, mesh=mesh, in_specs=in_specs, out_specs=P("ctx", "chan"), check_vma=False)
```
